32 devices in a mesh: tm: 4 (over x, core), space: 8 (over z, y).
Axes of the slice: x: 2, y: 2, z: 4, core: 2. Of those that a mesh axis runs over, the one named last changes fastest.
Arguments:
- snapshots: bfloat16 [1008, 5, 16, 8, 128], P('tm', None, 'space'), may hold values from -6 to 6
- picks: int32 [896], P('tm'), may hold values from 0 to 251, as said below
- basis: bfloat16 [32, 5, 16, 8, 128], P(None, None, 'space'), may hold values from -0.0390625 to 0.0390625
- kappa: float32 [5, 16, 8, 128], P(None, 'space'), may hold values from 0.03 to 0.16
Outputs:
- coefficients: float32 [896, 32], P('tm')
- factor: float32 [561, 561], replicated
The draws below stay inside these ranges and needn't reach their ends.
Inputs may be any that keep to these rules, and one draw needn't show every extreme that they name: `picks`: within each time group's 224 consecutive entries the indices are distinct, and 0 and 251 both occur.
All inputs are finite; a program needn't handle non-finite values.
Results may differ from the reference program's by a relative error of at most 0.0003.
Values may be sent and summed in bfloat16 or wider, within the bound.
A program may use at most 64 MiB of HBM per device.

```python
import math
import jax
import jax.numpy as jnp
import numpy as np
from jax import lax

MODES = 32
VARS = 5
NY = 8
NZ = 128
PICKS = 224
STORED = 252
TIME = 896
NX = 16
N_TM = 4


def draw_picks(key, part):
    groups = TIME // PICKS

    def one_group(group_key):
        first_key, second_key = jax.random.split(group_key)
        inner = jax.random.permutation(first_key, STORED - 2)[:PICKS - 2] + 1
        ends = jnp.array([0, STORED - 1], dtype=jnp.int32)
        row = jnp.concatenate([ends, inner.astype(jnp.int32)])
        return jax.random.permutation(second_key, row)
    keys = jax.random.split(jax.random.fold_in(key, 7), groups)
    return jax.vmap(one_group)(keys).reshape(-1).astype(jnp.int32)


def shard_levels(own_key, extent, cuts, low, largest):
    factor_of = 1.0
    for position, parts in cuts:
        heights = jax.random.uniform(jax.random.fold_in(jax.random.fold_in(own_key, 6), position), (parts,), jnp.float32, low / len(cuts), largest / len(cuts))
        factor_of = factor_of * jnp.repeat(jnp.exp(heights), extent[position] // parts).reshape((-1,) + (1,) * (len(extent) - 1 - position))
    return factor_of


def bell_draw(stream_key, extent, scale, limit, cuts=(), kind=jnp.bfloat16):
    values = jax.random.normal(stream_key, extent, jnp.float32) * scale
    if len(cuts) > 0:
        values = shard_levels(stream_key, extent, cuts, -0.22, 0.18) * values
    return jnp.clip(values, min=-limit, max=limit).astype(kind)


def setup_inputs(seed: int = 0) -> dict:
    streams_of = jax.random.split(jax.random.key(seed), 5)
    snapshots = bell_draw(streams_of[0], (STORED * N_TM, VARS, NX, NY, NZ), 1.0, 6.0, ((0, 4), (2, 8)))
    picks = draw_picks(jax.random.fold_in(streams_of[4], 71), 0)
    basis = bell_draw(streams_of[2], (MODES, VARS, NX, NY, NZ), (VARS * NX * NY * NZ // 4) ** -0.5, 0.0390625, ((2, 8),))
    kappa = jnp.clip(jnp.exp(math.log(0.16) - 1.6739764 * jax.random.uniform(streams_of[3], (VARS, NX, NY, NZ), jnp.float32) ** shard_levels(streams_of[3], (VARS, NX, NY, NZ), ((1, 8),), -0.2, 0.2)), 0.03, 0.16)
    return {"snapshots": snapshots, "picks": picks, "basis": basis, "kappa": kappa}


def smooth(field, kappa):
    padded = jnp.pad(field, ((0, 0), (1, 1), (1, 1), (1, 1)))
    beside = padded[:, 2:, 1:-1, 1:-1] + padded[:, :-2, 1:-1, 1:-1]
    beside = beside + padded[:, 1:-1, 2:, 1:-1] + padded[:, 1:-1, :-2, 1:-1]
    beside = beside + padded[:, 1:-1, 1:-1, 2:] + padded[:, 1:-1, 1:-1, :-2]
    return field + kappa * (beside - 6.0 * field)

def expand(coeffs):
    count = coeffs.shape[1]
    first, second = np.triu_indices(count)
    quad = coeffs[:, first] * coeffs[:, second]
    ones = jnp.ones((coeffs.shape[0], 1), coeffs.dtype)
    return jnp.concatenate([ones, coeffs, quad], axis=1)

def reference(snapshots, picks, basis, kappa):
    basis_flat = basis.astype(jnp.float32).reshape(basis.shape[0], -1)
    steps_all = jnp.arange(TIME, dtype=jnp.int32)

    def one_row(pair):
        step, pick = pair
        source = (step // PICKS * STORED + pick).astype(jnp.int32)
        taken = lax.dynamic_index_in_dim(snapshots, source, 0, keepdims=False)
        filtered = smooth(taken.astype(jnp.float32), kappa)
        flat = filtered.reshape(-1)
        return jnp.dot(basis_flat, flat, precision=lax.Precision.HIGHEST)
    coefficients = lax.map(one_row, (steps_all, picks))
    features = expand(coefficients)
    gram = jnp.dot(features.T, features, precision=lax.Precision.HIGHEST) / TIME
    factor = jnp.linalg.cholesky(gram).T
    return (coefficients, factor)
```

```python
import functools

import jax
import jax.numpy as jnp
import numpy as np
from jax import lax
from jax.experimental import pallas as pl
from jax.experimental.pallas import tpu as pltpu
from jax.sharding import PartitionSpec as P

MESH = pl.DeviceIdType.MESH
HIGHEST = lax.Precision.HIGHEST
NT = (((1,), (1,)), ((), ()))
TN = (((0,), (0,)), ((), ()))
CHUNK = 64
F32 = jnp.float32
BF16 = jnp.bfloat16


def project_kernel(count, s_ref, b_ref, k_ref, low_ref, high_ref, picks_ref, out_ref, g_ref, acc_ref):
    step = pl.program_id(0)
    modes, nv, nx, ny, nz = b_ref.shape
    wide = modes * ny

    @pl.when(step == 0)
    def _():
        acc_ref[...] = jnp.zeros_like(acc_ref)
        yi = lax.broadcasted_iota(jnp.int32, (wide, nz), 0) % ny
        zi = lax.broadcasted_iota(jnp.int32, (wide, nz), 1)

        def spread(plane):
            return jnp.broadcast_to(plane[None], (modes, ny, nz)).reshape(wide, nz)

        for v in range(nv):
            b = [b_ref[:, v, x].astype(F32).reshape(wide, nz) for x in range(nx)]
            kap = [spread(k_ref[v, x]) for x in range(nx)]
            w = [b[x] * kap[x] for x in range(nx)]
            sides = []
            for ref in (low_ref, high_ref):
                kn = ref[modes, v].astype(F32) + ref[modes + 1, v].astype(F32) + ref[modes + 2, v].astype(F32)
                sides.append(ref[:modes, v].astype(F32).reshape(wide, nz) * spread(kn))
            for x in range(nx):
                beside = (w[x - 1] if x > 0 else sides[0]) + (w[x + 1] if x < nx - 1 else sides[1])
                beside = beside + jnp.where(yi < ny - 1, pltpu.roll(w[x], wide - 1, 0), 0.0)
                beside = beside + jnp.where(yi > 0, pltpu.roll(w[x], 1, 0), 0.0)
                beside = beside + jnp.where(zi < nz - 1, pltpu.roll(w[x], nz - 1, 1), 0.0)
                beside = beside + jnp.where(zi > 0, pltpu.roll(w[x], 1, 1), 0.0)
                g = b[x] * (1.0 - 6.0 * kap[x]) + beside
                hi = g.astype(BF16)
                lo = (g - hi.astype(F32)).astype(BF16)
                at = pl.ds((v * nx + x) * nz, nz)
                g_ref[pl.ds(0, wide), at] = hi
                g_ref[pl.ds(wide, wide), at] = lo

    rows = jnp.concatenate(
        [s_ref[:, v, x].reshape(CHUNK * ny, nz) for v in range(nv) for x in range(nx)], axis=1
    )
    both = lax.dot_general(rows, g_ref[...], NT, preferred_element_type=F32)
    prod = both[:, :wide] + both[:, wide:]
    yr = lax.broadcasted_iota(jnp.int32, prod.shape, 0) % ny
    yc = lax.broadcasted_iota(jnp.int32, prod.shape, 1) % ny
    z = jnp.sum(jnp.where(yr == yc, prod, 0.0).reshape(CHUNK, ny, wide), axis=1)
    at = lax.broadcasted_iota(jnp.int32, z.shape, 0) + step * CHUNK
    z = jnp.where(at < count, z, 0.0)
    fold = (
        lax.broadcasted_iota(jnp.int32, (modes, wide), 1) // ny
        == lax.broadcasted_iota(jnp.int32, (modes, wide), 0)
    ).astype(F32)
    part = lax.dot_general(fold, z, NT, precision=HIGHEST, preferred_element_type=F32)
    lanes = acc_ref.shape[1]
    hot = (
        lax.broadcasted_iota(jnp.int32, (CHUNK, lanes), 0) + step * CHUNK
        == jnp.broadcast_to(picks_ref[...], (CHUNK, lanes))
    ).astype(F32)
    acc_ref[...] += jnp.dot(part, hot, precision=HIGHEST, preferred_element_type=F32)

    @pl.when(step == pl.num_programs(0) - 1)
    def _():
        halves = lanes // 128
        for i in range(modes // 8):
            for h in range(halves):
                out_ref[i * halves + h] = acc_ref[pl.ds(8 * i, 8), pl.ds(128 * h, 128)]


def project(snapshots, basis, kappa, low, high, picks_row):
    count, nv, nx, ny, nz = snapshots.shape
    modes = basis.shape[0]
    lanes = picks_row.shape[1]
    chunks = (modes // 8) * (lanes // 128)
    whole = lambda a: pl.BlockSpec(a.shape, lambda i: (0,) * a.ndim)
    return pl.pallas_call(
        functools.partial(project_kernel, count),
        grid=(-(-count // CHUNK),),
        out_shape=jax.ShapeDtypeStruct((chunks, 8, 128), F32),
        in_specs=[
            pl.BlockSpec((CHUNK, nv, nx, ny, nz), lambda i: (i, 0, 0, 0, 0)),
            whole(basis), whole(kappa), whole(low), whole(high), whole(picks_row),
        ],
        out_specs=pl.BlockSpec((chunks, 8, 128), lambda i: (0, 0, 0)),
        scratch_shapes=[
            pltpu.VMEM((2 * modes * ny, nv * nx * nz), BF16),
            pltpu.VMEM((modes, lanes), F32),
        ],
        compiler_params=pltpu.CompilerParams(vmem_limit_bytes=48 * 2**20),
        name="project",
    )(snapshots, basis, kappa, low, high, picks_row)


def share_kernel(n_tm, n_space, own_ref, all_ref, land_ref, send1, recv1, send2, recv2):
    chunks = own_ref.shape[0]
    tm = lax.axis_index("tm")
    sp = lax.axis_index("space")
    me = tm * n_space + sp
    total = n_tm * n_space

    def peer(i):
        other = lax.rem(me + i, total)
        return other // n_space, lax.rem(other, n_space)

    barrier = pltpu.get_barrier_semaphore()

    def greet(i, carry):
        pl.semaphore_signal(barrier, inc=1, device_id=peer(i), device_id_type=MESH)
        return carry

    lax.fori_loop(1, total, greet, 0)
    pl.semaphore_wait(barrier, total - 1)

    def part_to(owner):
        return pltpu.make_async_remote_copy(
            src_ref=own_ref.at[owner], dst_ref=land_ref.at[sp],
            send_sem=send1.at[owner], recv_sem=recv1.at[sp],
            device_id=(tm, owner), device_id_type=MESH,
        )

    def part_from(source):
        return pltpu.make_async_remote_copy(
            src_ref=own_ref.at[0], dst_ref=land_ref.at[source],
            send_sem=send1.at[0], recv_sem=recv1.at[source],
            device_id=(tm, source), device_id_type=MESH,
        )

    for owner in range(chunks):
        @pl.when(sp != owner)
        def _():
            part_to(owner).start()

    @pl.when(sp < chunks)
    def _():
        land_ref[sp] = own_ref[sp]
        for source in range(n_space):
            @pl.when(sp != source)
            def _():
                part_from(source).wait_recv()
        total_sum = land_ref[0]
        for source in range(1, n_space):
            total_sum = total_sum + land_ref[source]
        all_ref[tm, sp] = total_sum

        def give(i, carry):
            pltpu.make_async_remote_copy(
                src_ref=all_ref.at[tm, sp], dst_ref=all_ref.at[tm, sp],
                send_sem=send2.at[i], recv_sem=recv2.at[tm * chunks + sp],
                device_id=peer(i), device_id_type=MESH,
            ).start()
            return carry

        lax.fori_loop(1, total, give, 0)

    for owner in range(chunks):
        @pl.when(sp != owner)
        def _():
            part_to(owner).wait_send()

    for group in range(n_tm):
        for owner in range(chunks):
            @pl.when(jnp.logical_or(tm != group, sp != owner))
            def _():
                pltpu.make_async_remote_copy(
                    src_ref=all_ref.at[group, owner], dst_ref=all_ref.at[group, owner],
                    send_sem=send2.at[0], recv_sem=recv2.at[group * chunks + owner],
                    device_id=(group, owner), device_id_type=MESH,
                ).wait_recv()

    @pl.when(sp < chunks)
    def _():
        def done(i, carry):
            pltpu.make_async_remote_copy(
                src_ref=all_ref.at[tm, sp], dst_ref=all_ref.at[tm, sp],
                send_sem=send2.at[i], recv_sem=recv2.at[tm * chunks + sp],
                device_id=peer(i), device_id_type=MESH,
            ).wait_send()
            return carry

        lax.fori_loop(1, total, done, 0)


def share(own, n_tm, n_space):
    chunks = own.shape[0]
    total = n_tm * n_space
    return pl.pallas_call(
        functools.partial(share_kernel, n_tm, n_space),
        out_shape=jax.ShapeDtypeStruct((n_tm, chunks, 8, 128), F32),
        in_specs=[pl.BlockSpec(memory_space=pltpu.VMEM)],
        out_specs=pl.BlockSpec(memory_space=pltpu.VMEM),
        scratch_shapes=[
            pltpu.VMEM((n_space, 8, 128), F32),
            pltpu.SemaphoreType.DMA((chunks,)),
            pltpu.SemaphoreType.DMA((n_space,)),
            pltpu.SemaphoreType.DMA((total,)),
            pltpu.SemaphoreType.DMA((n_tm * chunks,)),
        ],
        compiler_params=pltpu.CompilerParams(collective_id=0, has_side_effects=True),
        name="share",
    )(own)


def eliminate(a, b):
    tiles = len(a)
    sub = lax.broadcasted_iota(jnp.int32, (8, 128), 0)
    row_of = lambda x, k: jnp.broadcast_to(x[k : k + 1, :], (8, 128))
    column_of = lambda x, k: jnp.broadcast_to(x[:, k : k + 1], (8, 128))
    diag = []
    for s in range(tiles):
        cols = [column_of(a[s], 8 * s + k) for k in range(8)]
        inv, known, a_rows, b_rows = [], [], [], []
        d = jnp.ones((8, 128), F32)
        for k in range(8):
            pivot = row_of(cols[k], k)
            d = jnp.where(sub == k, pivot, d)
            r = 1.0 / pivot
            m = jnp.where(sub > k, cols[k] * r, 0.0)
            seen = {}
            for q in range(k + 1, 8):
                seen[q] = row_of(cols[q], k)
                cols[q] = cols[q] - m * seen[q]
            a_rows.append(row_of(a[s], k))
            a[s] = a[s] - m * a_rows[k]
            if b is not None:
                b_rows.append(row_of(b[s], k))
                b[s] = b[s] - m * b_rows[k]
            inv.append(r)
            known.append(seen)
        diag.append(d)
        for i in range(s + 1, tiles):
            cols = [column_of(a[i], 8 * s + k) for k in range(8)]
            for k in range(8):
                m = cols[k] * inv[k]
                for q in range(k + 1, 8):
                    cols[q] = cols[q] - m * known[k][q]
                a[i] = a[i] - m * a_rows[k]
                if b is not None:
                    b[i] = b[i] - m * b_rows[k]
    scale = []
    for d in diag:
        y = lax.rsqrt(d)
        scale.append(y * (1.5 - 0.5 * d * y * y))
    return a, b, scale


def factor_kernel(count, n_feat, all_ref, s1_ref, s2_ref, c_ref, o_ref, f_ref, a_ref, u_ref, l_ref):
    n_tm, chunks = all_ref.shape[:2]
    padded = s1_ref.shape[0]
    blocks = padded // 128
    halves = -(-count // 128)
    lanes = halves * 128
    groups = chunks // halves
    modes = 8 * groups
    tm = lax.axis_index("tm")

    def coeffs(g):
        return jnp.concatenate(
            [
                jnp.concatenate([all_ref[g, i * halves + h] for h in range(halves)], axis=1)
                for i in range(groups)
            ],
            axis=0,
        )

    c_ref[...] = jnp.transpose(coeffs(tm))[:count, :]
    lane = lax.broadcasted_iota(jnp.int32, (modes, lanes), 1)
    top = lax.broadcasted_iota(jnp.int32, (modes, lanes), 0)
    ones = jnp.where(jnp.logical_and(lane < count, top == 0), 1.0, 0.0).astype(BF16)
    for g in range(n_tm):
        c = coeffs(g)
        hi = c.astype(BF16)
        rest = c - hi.astype(F32)
        mid = rest.astype(BF16)
        low = (rest - mid.astype(F32)).astype(BF16)
        stack = jnp.concatenate([hi, mid, low, ones], axis=0)
        f1 = jnp.dot(s1_ref[...], stack, preferred_element_type=F32)
        f2 = jnp.dot(s2_ref[...], stack, preferred_element_type=F32)
        f_ref[:, pl.ds(g * lanes, lanes)] = f1 * f2

    share_of = 1.0 / (count * n_tm)
    for j in range(blocks):
        gram = lax.dot_general(
            f_ref[pl.ds(j * 128, 128), :], f_ref[pl.ds(j * 128, padded - j * 128), :], NT,
            precision=HIGHEST, preferred_element_type=F32,
        )
        a_ref[pl.ds(j * 128, 128), pl.ds(j * 128, padded - j * 128)] = gram * share_of

    last = (blocks - 1) * 128
    ri = lax.broadcasted_iota(jnp.int32, (128, 128), 0)
    ci = lax.broadcasted_iota(jnp.int32, (128, 128), 1)
    corner = a_ref[pl.ds(last, 128), pl.ds(last, 128)]
    a_ref[pl.ds(last, 128), pl.ds(last, 128)] = corner + jnp.where(
        jnp.logical_and(ri == ci, ri + last >= n_feat), 1.0, 0.0
    )

    lane8 = lax.broadcasted_iota(jnp.int32, (8, 128), 1)
    sub8 = lax.broadcasted_iota(jnp.int32, (8, 128), 0)

    def block(j, carry):
        start = pl.multiple_of(j * 128, 128)
        a = [a_ref[pl.ds(start + 8 * i, 8), pl.ds(start, 128)] for i in range(16)]
        b = [jnp.where(lane8 == sub8 + 8 * i, 1.0, 0.0) for i in range(16)]
        a, b, scale = eliminate(a, b)
        for i in range(16):
            u_ref[pl.ds(8 * i, 8), :] = jnp.where(lane8 >= sub8 + 8 * i, a[i] * scale[i], 0.0)
            l_ref[pl.ds(8 * i, 8), :] = b[i] * scale[i]

        for jj in range(blocks - 1):
            @pl.when(j == jj)
            def _():
                here, after = jj * 128, (jj + 1) * 128
                if jj > 0:
                    o_ref[pl.ds(here, 128), pl.ds(0, here)] = jnp.zeros((128, here), F32)
                o_ref[pl.ds(here, 128), pl.ds(here, 128)] = u_ref[...]
                w = jnp.dot(
                    l_ref[...], a_ref[pl.ds(here, 128), pl.ds(after, padded - after)],
                    precision=HIGHEST, preferred_element_type=F32,
                )
                o_ref[pl.ds(here, 128), pl.ds(after, n_feat - after)] = w[:, : n_feat - after]
                for i in range(jj + 1, blocks):
                    row = i * 128
                    a_ref[pl.ds(row, 128), pl.ds(row, padded - row)] -= lax.dot_general(
                        w[:, row - after : row - after + 128], w[:, row - after :], TN,
                        precision=HIGHEST, preferred_element_type=F32,
                    )
        return carry

    lax.fori_loop(0, blocks - 1, block, 0)
    left = n_feat - last
    tiles = -(-left // 8)
    a = [a_ref[pl.ds(last + 8 * i, 8), pl.ds(last, 128)] for i in range(tiles)]
    a, _, scale = eliminate(a, None)
    for i in range(tiles):
        u_ref[pl.ds(8 * i, 8), :] = jnp.where(lane8 >= sub8 + 8 * i, a[i] * scale[i], 0.0)
    o_ref[pl.ds(last, left), pl.ds(0, last)] = jnp.zeros((left, last), F32)
    o_ref[pl.ds(last, left), pl.ds(last, left)] = u_ref[pl.ds(0, left), pl.ds(0, left)]


def selections(modes):
    first, second = np.triu_indices(modes)
    n_feat = 1 + modes + len(first)
    padded = -(-n_feat // 128) * 128
    one = 3 * modes
    s1 = np.zeros((padded, 4 * modes), np.float32)
    s2 = np.zeros((padded, 4 * modes), np.float32)
    s1[0, one] = s2[0, one] = 1.0
    for part in range(3):
        for m in range(modes):
            s1[1 + m, part * modes + m] = 1.0
        s1[1 + modes + np.arange(len(first)), part * modes + first] = 1.0
        s2[1 + modes + np.arange(len(first)), part * modes + second] = 1.0
    s2[1 : 1 + modes, one] = 1.0
    return n_feat, padded, s1, s2


def factorize(shared, count, modes):
    n_tm = shared.shape[0]
    n_feat, padded, s1, s2 = selections(modes)
    lanes = -(-count // 128) * 128
    vmem = pl.BlockSpec(memory_space=pltpu.VMEM)
    return pl.pallas_call(
        functools.partial(factor_kernel, count, n_feat),
        out_shape=(
            jax.ShapeDtypeStruct((count, modes), F32),
            jax.ShapeDtypeStruct((n_feat, n_feat), F32),
        ),
        in_specs=[vmem] * 3,
        out_specs=(vmem, vmem),
        scratch_shapes=[
            pltpu.VMEM((padded, n_tm * lanes), F32),
            pltpu.VMEM((padded, padded), F32),
            pltpu.VMEM((128, 128), F32),
            pltpu.VMEM((128, 128), F32),
        ],
        compiler_params=pltpu.CompilerParams(vmem_limit_bytes=48 * 2**20),
        name="factorize",
    )(shared, jnp.asarray(s1, BF16), jnp.asarray(s2, BF16))


def body(snapshots, picks, basis, kappa):
    n_tm, n_space = lax.axis_size("tm"), lax.axis_size("space")
    modes, count = basis.shape[0], picks.shape[0]
    hi = lax.reduce_precision(kappa, 8, 7)
    mid = lax.reduce_precision(kappa - hi, 8, 7)
    low = kappa - hi - mid
    parts = jnp.stack([hi, mid, low]).astype(BF16)

    def plane(x):
        return jnp.concatenate([basis[:, :, x], parts[:, :, x]], axis=0)

    forward = [(i, i + 1) for i in range(n_space - 1)]
    backward = [(i + 1, i) for i in range(n_space - 1)]
    from_low = lax.ppermute(plane(basis.shape[2] - 1), "space", forward)
    from_high = lax.ppermute(plane(0), "space", backward)
    lanes = -(-count // 128) * 128
    picks_row = jnp.pad(picks, (0, lanes - count), constant_values=-1).reshape(1, lanes)
    own = project(snapshots, basis, kappa, from_low, from_high, picks_row)
    shared = share(own, n_tm, n_space)
    return tuple(factorize(shared, count, modes))


def solution(mesh):
    in_specs = (
        P("tm", None, "space", None, None),
        P("tm"),
        P(None, None, "space", None, None),
        P(None, "space", None, None),
    )
    out_specs = (P("tm", None), P())
    return jax.shard_map(body, mesh=mesh, in_specs=in_specs, out_specs=out_specs, check_vma=False)
```

```python
import functools

import jax
import jax.numpy as jnp
import numpy as np
from jax import lax
from jax.experimental import pallas as pl
from jax.experimental.pallas import tpu as pltpu
from jax.sharding import PartitionSpec as P

MESH = pl.DeviceIdType.MESH
HIGHEST = lax.Precision.HIGHEST
NT = (((1,), (1,)), ((), ()))
TN = (((0,), (0,)), ((), ()))
CHUNK = 64
F32 = jnp.float32
BF16 = jnp.bfloat16


def gather_kernel(
    n_tm, n_space, chunks, s_any, b_ref, k_ref, picks_ref, all_ref,
    s_ref, g_ref, z_ref, hb_ref, hk_ref, own_ref, land_ref,
    load, send_b, recv_b, send_k, recv_k, send_f, recv_f, send1, recv1, send2, recv2,
):
    count, nv, nx, ny, nz = s_any.shape
    modes = b_ref.shape[0]
    wide, half = modes * ny, modes // 2
    lanes = picks_ref.shape[1]
    rows_all = s_ref.shape[0]
    tm = lax.axis_index("tm")
    sp = lax.axis_index("space")
    core = lax.rem(tm, 2)
    sibling = tm + 1 - 2 * core
    me = tm * n_space + sp
    total = n_tm * n_space

    def peer(i):
        other = lax.rem(me + i, total)
        return other // n_space, lax.rem(other, n_space)

    loading = pltpu.make_async_copy(s_any, s_ref.at[pl.ds(0, count)], load)
    loading.start()
    barrier = pltpu.get_barrier_semaphore()

    def greet(i, carry):
        pl.semaphore_signal(barrier, inc=1, device_id=peer(i), device_id_type=MESH)
        return carry

    lax.fori_loop(1, total, greet, 0)
    pl.semaphore_wait(barrier, total - 1)

    def remote(src, dst, send, recv, device):
        return pltpu.make_async_remote_copy(
            src_ref=src, dst_ref=dst, send_sem=send, recv_sem=recv,
            device_id=device, device_id_type=MESH,
        )

    def plane_copies(side):
        x = nx - 1 if side == 0 else 0
        to = lax.rem(sp + (1 if side == 0 else n_space - 1), n_space)
        mine = pl.ds(core * half, half)
        return (
            remote(b_ref.at[mine, :, x], hb_ref.at[side, mine], send_b.at[side], recv_b.at[side], (tm, to)),
            remote(k_ref.at[:, x], hk_ref.at[side], send_k.at[side], recv_k.at[side], (tm, to)),
        )

    def forward(side):
        mine = pl.ds(core * half, half)
        return remote(
            hb_ref.at[side, mine], hb_ref.at[side, mine], send_f.at[side], recv_f.at[side], (sibling, sp)
        )

    sends = (sp < n_space - 1, sp > 0)
    receives = (sp > 0, sp < n_space - 1)
    for side in range(2):
        @pl.when(sends[side])
        def _():
            for copy in plane_copies(side):
                copy.start()

        @pl.when(jnp.logical_not(receives[side]))
        def _():
            hb_ref[side] = jnp.zeros(hb_ref.shape[1:], BF16)
            hk_ref[side] = jnp.zeros(hk_ref.shape[1:], F32)

    def store(g, at_row, v, x):
        size = g.shape[0]
        hi = g.astype(BF16)
        lo = (g - hi.astype(F32)).astype(BF16)
        at = pl.ds((v * nx + x) * nz, nz)
        g_ref[pl.ds(at_row, size), at] = hi
        g_ref[pl.ds(wide + at_row, size), at] = lo

    def spread(plane, many):
        return jnp.broadcast_to(plane[None], (many, ny, nz)).reshape(many * ny, nz)

    yi = lax.broadcasted_iota(jnp.int32, (wide, nz), 0) % ny
    zi = lax.broadcasted_iota(jnp.int32, (wide, nz), 1)
    for v in range(nv):
        b = [b_ref[:, v, x].astype(F32).reshape(wide, nz) for x in range(nx)]
        kap = [spread(k_ref[v, x], modes) for x in range(nx)]
        w = [b[x] * kap[x] for x in range(nx)]
        for x in range(nx):
            g = b[x] * (1.0 - 6.0 * kap[x])
            if x > 0:
                g = g + w[x - 1]
            if x < nx - 1:
                g = g + w[x + 1]
            g = g + jnp.where(yi < ny - 1, pltpu.roll(w[x], wide - 1, 0), 0.0)
            g = g + jnp.where(yi > 0, pltpu.roll(w[x], 1, 0), 0.0)
            g = g + jnp.where(zi < nz - 1, pltpu.roll(w[x], nz - 1, 1), 0.0)
            g = g + jnp.where(zi > 0, pltpu.roll(w[x], 1, 1), 0.0)
            store(g, 0, v, x)

    if rows_all > count:
        s_ref[pl.ds(count, rows_all - count)] = jnp.zeros((rows_all - count,) + s_ref.shape[1:], BF16)
    loading.wait()

    yr = lax.broadcasted_iota(jnp.int32, (CHUNK * ny, wide), 0) % ny
    yc = lax.broadcasted_iota(jnp.int32, (CHUNK * ny, wide), 1) % ny

    def contract(i):
        at = pl.ds(i * CHUNK, CHUNK)
        rows = jnp.concatenate(
            [s_ref[at, v, x].reshape(CHUNK * ny, nz) for v in range(nv) for x in range(nx)], axis=1
        )
        both = lax.dot_general(rows, g_ref[...], NT, preferred_element_type=F32)
        prod = both[:, :wide] + both[:, wide:]
        return jnp.sum(jnp.where(yr == yc, prod, 0.0).reshape(CHUNK, ny, wide), axis=1)

    def inner(i, carry):
        z_ref[pl.ds(pl.multiple_of(i * CHUNK, CHUNK), CHUNK), :] = contract(i)
        return carry

    lax.fori_loop(0, rows_all // CHUNK, inner, 0)

    for side in range(2):
        @pl.when(receives[side])
        def _():
            for copy in plane_copies(side):
                copy.wait_recv()
            forward(side).start()

    def outer_modes(which):
        row = pl.multiple_of(which * (half * ny), half * ny)
        for v in range(nv):
            for side, x in ((0, 0), (1, nx - 1)):
                plane = hb_ref[side, pl.ds(which * half, half), v].astype(F32).reshape(half * ny, nz)
                store(plane * spread(hk_ref[side, v], half), row, v, x)

    outer_modes(core)
    for side in range(2):
        @pl.when(receives[side])
        def _():
            forward(side).wait_recv()
    outer_modes(1 - core)

    def outer(i, carry):
        z_ref[pl.ds(pl.multiple_of(i * CHUNK, CHUNK), CHUNK), :] += contract(i)
        return carry

    lax.fori_loop(0, rows_all // CHUNK, outer, 0)

    fold = (
        lax.broadcasted_iota(jnp.int32, (modes, wide), 1) // ny
        == lax.broadcasted_iota(jnp.int32, (modes, wide), 0)
    ).astype(F32)
    part = lax.dot_general(fold, z_ref[...], NT, precision=HIGHEST, preferred_element_type=F32)
    hot = (
        lax.broadcasted_iota(jnp.int32, (rows_all, lanes), 0)
        == jnp.broadcast_to(picks_ref[...], (rows_all, lanes))
    ).astype(F32)
    mine = jnp.dot(part, hot, precision=HIGHEST, preferred_element_type=F32)
    halves = lanes // 128
    for i in range(modes // 8):
        for h in range(halves):
            own_ref[i * halves + h] = mine[8 * i : 8 * i + 8, 128 * h : 128 * h + 128]

    def part_to(owner):
        return remote(own_ref.at[owner], land_ref.at[sp], send1.at[owner], recv1.at[sp], (tm, owner))

    for owner in range(chunks):
        @pl.when(sp != owner)
        def _():
            part_to(owner).start()

    def give_to(i):
        return remote(
            all_ref.at[tm, sp], all_ref.at[tm, sp], send2.at[i], recv2.at[tm * chunks + sp], peer(i)
        )

    @pl.when(sp < chunks)
    def _():
        land_ref[sp] = own_ref[sp]
        for source in range(n_space):
            @pl.when(sp != source)
            def _():
                remote(
                    own_ref.at[0], land_ref.at[source], send1.at[0], recv1.at[source], (tm, source)
                ).wait_recv()
        total_sum = land_ref[0]
        for source in range(1, n_space):
            total_sum = total_sum + land_ref[source]
        all_ref[tm, sp] = total_sum

        def give(i, carry):
            give_to(i).start()
            return carry

        lax.fori_loop(1, total, give, 0)

    for side in range(2):
        @pl.when(sends[side])
        def _():
            for copy in plane_copies(side):
                copy.wait_send()

        @pl.when(receives[side])
        def _():
            forward(side).wait_send()

    for owner in range(chunks):
        @pl.when(sp != owner)
        def _():
            part_to(owner).wait_send()

    for group in range(n_tm):
        for owner in range(chunks):
            @pl.when(jnp.logical_or(tm != group, sp != owner))
            def _():
                remote(
                    all_ref.at[group, owner], all_ref.at[group, owner],
                    send2.at[0], recv2.at[group * chunks + owner], (group, owner),
                ).wait_recv()

    @pl.when(sp < chunks)
    def _():
        def done(i, carry):
            give_to(i).wait_send()
            return carry

        lax.fori_loop(1, total, done, 0)


def gather_coefficients(snapshots, basis, kappa, picks_row, n_tm, n_space):
    count, nv, nx, ny, nz = snapshots.shape
    modes = basis.shape[0]
    lanes = picks_row.shape[1]
    chunks = (modes // 8) * (lanes // 128)
    rows_all = -(-count // CHUNK) * CHUNK
    vmem = pl.BlockSpec(memory_space=pltpu.VMEM)
    dma = pltpu.SemaphoreType.DMA
    return pl.pallas_call(
        functools.partial(gather_kernel, n_tm, n_space, chunks),
        out_shape=jax.ShapeDtypeStruct((n_tm, chunks, 8, 128), F32),
        in_specs=[pl.BlockSpec(memory_space=pl.ANY), vmem, vmem, vmem],
        out_specs=vmem,
        scratch_shapes=[
            pltpu.VMEM((rows_all, nv, nx, ny, nz), BF16),
            pltpu.VMEM((2 * modes * ny, nv * nx * nz), BF16),
            pltpu.VMEM((rows_all, modes * ny), F32),
            pltpu.VMEM((2, modes, nv, ny, nz), BF16),
            pltpu.VMEM((2, nv, ny, nz), F32),
            pltpu.VMEM((chunks, 8, 128), F32),
            pltpu.VMEM((n_space, 8, 128), F32),
            dma, dma((2,)), dma((2,)), dma((2,)), dma((2,)), dma((2,)), dma((2,)),
            dma((chunks,)), dma((n_space,)), dma((n_tm * n_space,)), dma((n_tm * chunks,)),
        ],
        compiler_params=pltpu.CompilerParams(
            collective_id=0, has_side_effects=True, vmem_limit_bytes=48 * 2**20
        ),
        name="gather_coefficients",
    )(snapshots, basis, kappa, picks_row)


def eliminate(a, b):
    tiles = len(a)
    sub = lax.broadcasted_iota(jnp.int32, (8, 128), 0)
    row_of = lambda x, k: jnp.broadcast_to(x[k : k + 1, :], (8, 128))
    column_of = lambda x, k: jnp.broadcast_to(x[:, k : k + 1], (8, 128))
    diag = []
    for s in range(tiles):
        cols = [column_of(a[s], 8 * s + k) for k in range(8)]
        inv, known, a_rows, b_rows = [], [], [], []
        d = jnp.ones((8, 128), F32)
        for k in range(8):
            pivot = row_of(cols[k], k)
            d = jnp.where(sub == k, pivot, d)
            r = 1.0 / pivot
            m = jnp.where(sub > k, cols[k] * r, 0.0)
            seen = {}
            for q in range(k + 1, 8):
                seen[q] = row_of(cols[q], k)
                cols[q] = cols[q] - m * seen[q]
            a_rows.append(row_of(a[s], k))
            a[s] = a[s] - m * a_rows[k]
            if b is not None:
                b_rows.append(row_of(b[s], k))
                b[s] = b[s] - m * b_rows[k]
            inv.append(r)
            known.append(seen)
        diag.append(d)
        for i in range(s + 1, tiles):
            cols = [column_of(a[i], 8 * s + k) for k in range(8)]
            for k in range(8):
                m = cols[k] * inv[k]
                for q in range(k + 1, 8):
                    cols[q] = cols[q] - m * known[k][q]
                a[i] = a[i] - m * a_rows[k]
                if b is not None:
                    b[i] = b[i] - m * b_rows[k]
    scale = []
    for d in diag:
        y = lax.rsqrt(d)
        scale.append(y * (1.5 - 0.5 * d * y * y))
    return a, b, scale


def factor_kernel(count, n_feat, all_ref, s1_ref, s2_ref, c_ref, o_ref, f_ref, a_ref, u_ref, l_ref):
    n_tm, chunks = all_ref.shape[:2]
    padded = s1_ref.shape[0]
    blocks = padded // 128
    halves = -(-count // 128)
    lanes = halves * 128
    groups = chunks // halves
    modes = 8 * groups
    tm = lax.axis_index("tm")

    def coeffs(g):
        return jnp.concatenate(
            [
                jnp.concatenate([all_ref[g, i * halves + h] for h in range(halves)], axis=1)
                for i in range(groups)
            ],
            axis=0,
        )

    c_ref[...] = jnp.transpose(coeffs(tm))[:count, :]
    lane = lax.broadcasted_iota(jnp.int32, (modes, lanes), 1)
    top = lax.broadcasted_iota(jnp.int32, (modes, lanes), 0)
    ones = jnp.where(jnp.logical_and(lane < count, top == 0), 1.0, 0.0).astype(BF16)
    for g in range(n_tm):
        c = coeffs(g)
        hi = c.astype(BF16)
        rest = c - hi.astype(F32)
        mid = rest.astype(BF16)
        low = (rest - mid.astype(F32)).astype(BF16)
        stack = jnp.concatenate([hi, mid, low, ones], axis=0)
        f1 = jnp.dot(s1_ref[...], stack, preferred_element_type=F32)
        f2 = jnp.dot(s2_ref[...], stack, preferred_element_type=F32)
        f_ref[:, pl.ds(g * lanes, lanes)] = f1 * f2

    share_of = 1.0 / (count * n_tm)
    for j in range(blocks):
        gram = lax.dot_general(
            f_ref[pl.ds(j * 128, 128), :], f_ref[pl.ds(j * 128, padded - j * 128), :], NT,
            precision=HIGHEST, preferred_element_type=F32,
        )
        a_ref[pl.ds(j * 128, 128), pl.ds(j * 128, padded - j * 128)] = gram * share_of

    last = (blocks - 1) * 128
    ri = lax.broadcasted_iota(jnp.int32, (128, 128), 0)
    ci = lax.broadcasted_iota(jnp.int32, (128, 128), 1)
    corner = a_ref[pl.ds(last, 128), pl.ds(last, 128)]
    a_ref[pl.ds(last, 128), pl.ds(last, 128)] = corner + jnp.where(
        jnp.logical_and(ri == ci, ri + last >= n_feat), 1.0, 0.0
    )

    lane8 = lax.broadcasted_iota(jnp.int32, (8, 128), 1)
    sub8 = lax.broadcasted_iota(jnp.int32, (8, 128), 0)

    def block(j, carry):
        start = pl.multiple_of(j * 128, 128)
        a = [a_ref[pl.ds(start + 8 * i, 8), pl.ds(start, 128)] for i in range(16)]
        b = [jnp.where(lane8 == sub8 + 8 * i, 1.0, 0.0) for i in range(16)]
        a, b, scale = eliminate(a, b)
        for i in range(16):
            u_ref[pl.ds(8 * i, 8), :] = jnp.where(lane8 >= sub8 + 8 * i, a[i] * scale[i], 0.0)
            l_ref[pl.ds(8 * i, 8), :] = b[i] * scale[i]

        for jj in range(blocks - 1):
            @pl.when(j == jj)
            def _():
                here, after = jj * 128, (jj + 1) * 128
                if jj > 0:
                    o_ref[pl.ds(here, 128), pl.ds(0, here)] = jnp.zeros((128, here), F32)
                o_ref[pl.ds(here, 128), pl.ds(here, 128)] = u_ref[...]
                w = jnp.dot(
                    l_ref[...], a_ref[pl.ds(here, 128), pl.ds(after, padded - after)],
                    precision=HIGHEST, preferred_element_type=F32,
                )
                o_ref[pl.ds(here, 128), pl.ds(after, n_feat - after)] = w[:, : n_feat - after]
                for i in range(jj + 1, blocks):
                    row = i * 128
                    a_ref[pl.ds(row, 128), pl.ds(row, padded - row)] -= lax.dot_general(
                        w[:, row - after : row - after + 128], w[:, row - after :], TN,
                        precision=HIGHEST, preferred_element_type=F32,
                    )
        return carry

    lax.fori_loop(0, blocks - 1, block, 0)
    left = n_feat - last
    tiles = -(-left // 8)
    a = [a_ref[pl.ds(last + 8 * i, 8), pl.ds(last, 128)] for i in range(tiles)]
    a, _, scale = eliminate(a, None)
    for i in range(tiles):
        u_ref[pl.ds(8 * i, 8), :] = jnp.where(lane8 >= sub8 + 8 * i, a[i] * scale[i], 0.0)
    o_ref[pl.ds(last, left), pl.ds(0, last)] = jnp.zeros((left, last), F32)
    o_ref[pl.ds(last, left), pl.ds(last, left)] = u_ref[pl.ds(0, left), pl.ds(0, left)]


def selections(modes):
    first, second = np.triu_indices(modes)
    n_feat = 1 + modes + len(first)
    padded = -(-n_feat // 128) * 128
    one = 3 * modes
    s1 = np.zeros((padded, 4 * modes), np.float32)
    s2 = np.zeros((padded, 4 * modes), np.float32)
    s1[0, one] = s2[0, one] = 1.0
    for part in range(3):
        for m in range(modes):
            s1[1 + m, part * modes + m] = 1.0
        s1[1 + modes + np.arange(len(first)), part * modes + first] = 1.0
        s2[1 + modes + np.arange(len(first)), part * modes + second] = 1.0
    s2[1 : 1 + modes, one] = 1.0
    return n_feat, padded, s1, s2


def factorize(shared, count, modes):
    n_tm = shared.shape[0]
    n_feat, padded, s1, s2 = selections(modes)
    lanes = -(-count // 128) * 128
    vmem = pl.BlockSpec(memory_space=pltpu.VMEM)
    return pl.pallas_call(
        functools.partial(factor_kernel, count, n_feat),
        out_shape=(
            jax.ShapeDtypeStruct((count, modes), F32),
            jax.ShapeDtypeStruct((n_feat, n_feat), F32),
        ),
        in_specs=[vmem] * 3,
        out_specs=(vmem, vmem),
        scratch_shapes=[
            pltpu.VMEM((padded, n_tm * lanes), F32),
            pltpu.VMEM((padded, padded), F32),
            pltpu.VMEM((128, 128), F32),
            pltpu.VMEM((128, 128), F32),
        ],
        compiler_params=pltpu.CompilerParams(vmem_limit_bytes=48 * 2**20),
        name="factorize",
    )(shared, jnp.asarray(s1, BF16), jnp.asarray(s2, BF16))


def body(snapshots, picks, basis, kappa):
    n_tm, n_space = lax.axis_size("tm"), lax.axis_size("space")
    modes, count = basis.shape[0], picks.shape[0]
    lanes = -(-count // 128) * 128
    picks_row = jnp.pad(picks, (0, lanes - count), constant_values=-1).reshape(1, lanes)
    shared = gather_coefficients(snapshots, basis, kappa, picks_row, n_tm, n_space)
    return tuple(factorize(shared, count, modes))


def solution(mesh):
    in_specs = (
        P("tm", None, "space", None, None),
        P("tm"),
        P(None, None, "space", None, None),
        P(None, "space", None, None),
    )
    out_specs = (P("tm", None), P())
    return jax.shard_map(body, mesh=mesh, in_specs=in_specs, out_specs=out_specs, check_vma=False)
```

```python
import functools

import jax
import jax.numpy as jnp
import numpy as np
from jax import lax
from jax.experimental import pallas as pl
from jax.experimental.pallas import tpu as pltpu
from jax.sharding import PartitionSpec as P

MESH = pl.DeviceIdType.MESH
HIGHEST = lax.Precision.HIGHEST
NT = (((1,), (1,)), ((), ()))
TN = (((0,), (0,)), ((), ()))
CHUNK = 128
F32 = jnp.float32
BF16 = jnp.bfloat16


def gather_kernel(
    n_tm, n_space, chunks, s_any, b_any, k_any, picks_ref, all_ref,
    s_ref, b_ref, k_ref, g_ref, z_ref, hb_ref, hk_ref, own_ref, land_ref,
    load, load_b, load_k, send_b, recv_b, send_k, recv_k, send_f, recv_f, send1, recv1, send2, recv2,
):
    count, nv, nx, ny, nz = s_any.shape
    modes = b_any.shape[0]
    wide, half = modes * ny, modes // 2
    taken = picks_ref.shape[1]
    rows_all = s_ref.shape[0]
    tm = lax.axis_index("tm")
    sp = lax.axis_index("space")
    core = lax.rem(tm, 2)
    sibling = tm + 1 - 2 * core
    me = tm * n_space + sp
    total = n_tm * n_space

    def peer(i):
        other = lax.rem(me + i, total)
        return other // n_space, lax.rem(other, n_space)

    loading_b = pltpu.make_async_copy(b_any, b_ref, load_b)
    loading_k = pltpu.make_async_copy(k_any, k_ref, load_k)
    loading_b.start()
    loading_k.start()
    loading = pltpu.make_async_copy(s_any, s_ref.at[pl.ds(0, count)], load)
    loading.start()
    barrier = pltpu.get_barrier_semaphore()

    def greet(i, carry):
        pl.semaphore_signal(barrier, inc=1, device_id=peer(i), device_id_type=MESH)
        return carry

    lax.fori_loop(1, total, greet, 0)
    pl.semaphore_wait(barrier, total - 1)

    def remote(src, dst, send, recv, device):
        return pltpu.make_async_remote_copy(
            src_ref=src, dst_ref=dst, send_sem=send, recv_sem=recv,
            device_id=device, device_id_type=MESH,
        )

    def plane_copies(side):
        x = nx - 1 if side == 0 else 0
        to = lax.rem(sp + (1 if side == 0 else n_space - 1), n_space)
        mine = pl.ds(core * half, half)
        return (
            remote(b_any.at[mine, :, x], hb_ref.at[side, mine], send_b.at[side], recv_b.at[side], (tm, to)),
            remote(k_any.at[:, x], hk_ref.at[side], send_k.at[side], recv_k.at[side], (tm, to)),
        )

    def forward(side):
        mine = pl.ds(core * half, half)
        return remote(
            hb_ref.at[side, mine], hb_ref.at[side, mine], send_f.at[side], recv_f.at[side], (sibling, sp)
        )

    sends = (sp < n_space - 1, sp > 0)
    receives = (sp > 0, sp < n_space - 1)
    for side in range(2):
        @pl.when(sends[side])
        def _():
            for copy in plane_copies(side):
                copy.start()

        @pl.when(jnp.logical_not(receives[side]))
        def _():
            hb_ref[side] = jnp.zeros(hb_ref.shape[1:], BF16)
            hk_ref[side] = jnp.zeros(hk_ref.shape[1:], F32)

    def store(g, at_row, v, x):
        size = g.shape[0]
        hi = g.astype(BF16)
        lo = (g - hi.astype(F32)).astype(BF16)
        at = pl.ds((v * nx + x) * nz, nz)
        g_ref[pl.ds(at_row, size), at] = hi
        g_ref[pl.ds(wide + at_row, size), at] = lo

    def spread(plane, many):
        return jnp.broadcast_to(plane[None], (many, ny, nz)).reshape(many * ny, nz)

    loading_b.wait()
    loading_k.wait()
    yi = lax.broadcasted_iota(jnp.int32, (wide, nz), 0) % ny
    zi = lax.broadcasted_iota(jnp.int32, (wide, nz), 1)
    for v in range(nv):
        b = [b_ref[:, v, x].astype(F32).reshape(wide, nz) for x in range(nx)]
        kap = [spread(k_ref[v, x], modes) for x in range(nx)]
        w = [b[x] * kap[x] for x in range(nx)]
        for x in range(nx):
            g = b[x] * (1.0 - 6.0 * kap[x])
            if x > 0:
                g = g + w[x - 1]
            if x < nx - 1:
                g = g + w[x + 1]
            g = g + jnp.where(yi < ny - 1, pltpu.roll(w[x], wide - 1, 0), 0.0)
            g = g + jnp.where(yi > 0, pltpu.roll(w[x], 1, 0), 0.0)
            g = g + jnp.where(zi < nz - 1, pltpu.roll(w[x], nz - 1, 1), 0.0)
            g = g + jnp.where(zi > 0, pltpu.roll(w[x], 1, 1), 0.0)
            store(g, 0, v, x)

    if rows_all > count:
        s_ref[pl.ds(count, rows_all - count)] = jnp.zeros((rows_all - count,) + s_ref.shape[1:], BF16)
    loading.wait()

    yr = lax.broadcasted_iota(jnp.int32, (CHUNK * ny, wide), 0) % ny
    yc = lax.broadcasted_iota(jnp.int32, (CHUNK * ny, wide), 1) % ny

    def contract(i):
        at = pl.ds(i * CHUNK, CHUNK)
        rows = jnp.concatenate(
            [s_ref[at, v, x].reshape(CHUNK * ny, nz) for v in range(nv) for x in range(nx)], axis=1
        )
        both = lax.dot_general(rows, g_ref[...], NT, preferred_element_type=F32)
        prod = both[:, :wide] + both[:, wide:]
        return jnp.sum(jnp.where(yr == yc, prod, 0.0).reshape(CHUNK, ny, wide), axis=1)

    def inner(i, carry):
        z_ref[pl.ds(pl.multiple_of(i * CHUNK, CHUNK), CHUNK), :] = contract(i)
        return carry

    lax.fori_loop(0, rows_all // CHUNK, inner, 0)

    for side in range(2):
        @pl.when(receives[side])
        def _():
            for copy in plane_copies(side):
                copy.wait_recv()
            forward(side).start()

    def outer_modes(which):
        row = pl.multiple_of(which * (half * ny), half * ny)
        for v in range(nv):
            for side, x in ((0, 0), (1, nx - 1)):
                plane = hb_ref[side, pl.ds(which * half, half), v].astype(F32).reshape(half * ny, nz)
                store(plane * spread(hk_ref[side, v], half), row, v, x)

    outer_modes(core)
    for side in range(2):
        @pl.when(receives[side])
        def _():
            forward(side).wait_recv()
    outer_modes(1 - core)

    def outer(i, carry):
        z_ref[pl.ds(pl.multiple_of(i * CHUNK, CHUNK), CHUNK), :] += contract(i)
        return carry

    lax.fori_loop(0, rows_all // CHUNK, outer, 0)

    fold = (
        lax.broadcasted_iota(jnp.int32, (modes, wide), 1) // ny
        == lax.broadcasted_iota(jnp.int32, (modes, wide), 0)
    ).astype(F32)
    part = lax.dot_general(fold, z_ref[...], NT, precision=HIGHEST, preferred_element_type=F32)
    hot = (
        lax.broadcasted_iota(jnp.int32, (rows_all, taken), 0)
        == jnp.broadcast_to(picks_ref[...], (rows_all, taken))
    ).astype(F32)
    mine = jnp.dot(part, hot, precision=HIGHEST, preferred_element_type=F32)
    halves = -(-taken // 128)
    for i in range(modes // 8):
        for h in range(halves):
            width = min(128, taken - 128 * h)
            if width < 128:
                own_ref[i * halves + h] = jnp.zeros((8, 128), F32)
            own_ref[i * halves + h, :, pl.ds(0, width)] = mine[8 * i : 8 * i + 8, 128 * h : 128 * h + width]

    def part_to(owner):
        return remote(own_ref.at[owner], land_ref.at[sp], send1.at[owner], recv1.at[sp], (tm, owner))

    for owner in range(chunks):
        @pl.when(sp != owner)
        def _():
            part_to(owner).start()

    def give_to(i):
        return remote(
            all_ref.at[tm, sp], all_ref.at[tm, sp], send2.at[i], recv2.at[tm * chunks + sp], peer(i)
        )

    @pl.when(sp < chunks)
    def _():
        land_ref[sp] = own_ref[sp]
        for source in range(n_space):
            @pl.when(sp != source)
            def _():
                remote(
                    own_ref.at[0], land_ref.at[source], send1.at[0], recv1.at[source], (tm, source)
                ).wait_recv()
        total_sum = land_ref[0]
        for source in range(1, n_space):
            total_sum = total_sum + land_ref[source]
        all_ref[tm, sp] = total_sum

        def give(i, carry):
            give_to(i).start()
            return carry

        lax.fori_loop(1, total, give, 0)

    for side in range(2):
        @pl.when(sends[side])
        def _():
            for copy in plane_copies(side):
                copy.wait_send()

        @pl.when(receives[side])
        def _():
            forward(side).wait_send()

    for owner in range(chunks):
        @pl.when(sp != owner)
        def _():
            part_to(owner).wait_send()

    for group in range(n_tm):
        for owner in range(chunks):
            @pl.when(jnp.logical_or(tm != group, sp != owner))
            def _():
                remote(
                    all_ref.at[group, owner], all_ref.at[group, owner],
                    send2.at[0], recv2.at[group * chunks + owner], (group, owner),
                ).wait_recv()

    @pl.when(sp < chunks)
    def _():
        def done(i, carry):
            give_to(i).wait_send()
            return carry

        lax.fori_loop(1, total, done, 0)


def gather_coefficients(snapshots, basis, kappa, picks_row, n_tm, n_space):
    count, nv, nx, ny, nz = snapshots.shape
    modes = basis.shape[0]
    chunks = (modes // 8) * -(-picks_row.shape[1] // 128)
    rows_all = -(-count // CHUNK) * CHUNK
    vmem = pl.BlockSpec(memory_space=pltpu.VMEM)
    dma = pltpu.SemaphoreType.DMA
    return pl.pallas_call(
        functools.partial(gather_kernel, n_tm, n_space, chunks),
        out_shape=jax.ShapeDtypeStruct((n_tm, chunks, 8, 128), F32),
        in_specs=[pl.BlockSpec(memory_space=pltpu.HBM)] * 3 + [vmem],
        out_specs=vmem,
        scratch_shapes=[
            pltpu.VMEM((rows_all, nv, nx, ny, nz), BF16),
            pltpu.VMEM(basis.shape, BF16),
            pltpu.VMEM(kappa.shape, F32),
            pltpu.VMEM((2 * modes * ny, nv * nx * nz), BF16),
            pltpu.VMEM((rows_all, modes * ny), F32),
            pltpu.VMEM((2, modes, nv, ny, nz), BF16),
            pltpu.VMEM((2, nv, ny, nz), F32),
            pltpu.VMEM((chunks, 8, 128), F32),
            pltpu.VMEM((n_space, 8, 128), F32),
            dma, dma, dma, dma((2,)), dma((2,)), dma((2,)), dma((2,)), dma((2,)), dma((2,)),
            dma((chunks,)), dma((n_space,)), dma((n_tm * n_space,)), dma((n_tm * chunks,)),
        ],
        compiler_params=pltpu.CompilerParams(
            collective_id=0, has_side_effects=True, vmem_limit_bytes=48 * 2**20
        ),
        name="gather_coefficients",
    )(snapshots, basis, kappa, picks_row)


def reciprocal(x):
    r = pl.reciprocal(x, approx=True)
    r = r * (2.0 - x * r)
    return r * (2.0 - x * r)


def eliminate(a, b):
    tiles = len(a)
    sub = lax.broadcasted_iota(jnp.int32, (8, 128), 0)
    row_of = lambda x, k: jnp.broadcast_to(x[k : k + 1, :], (8, 128))
    column_of = lambda x, k: jnp.broadcast_to(x[:, k : k + 1], (8, 128))
    diag = []
    for s in range(tiles):
        cols = [column_of(a[s], 8 * s + k) for k in range(8)]
        inv, known, a_rows, b_rows = [], [], [], []
        d = jnp.ones((8, 128), F32)
        e = jnp.ones((8, 128), F32)
        for k in range(8):
            pivot = row_of(cols[k], k)
            r = reciprocal(pivot)
            seen = {}
            for q in range(k + 1, 8):
                seen[q] = row_of(cols[q], k)
                cols[q] = cols[q] - (cols[k] * seen[q]) * r
            d = jnp.where(sub == k, pivot, d)
            e = jnp.where(sub == k, r, e)
            m = jnp.where(sub > k, cols[k] * r, 0.0)
            a_rows.append(row_of(a[s], k))
            a[s] = a[s] - m * a_rows[k]
            if b is not None:
                b_rows.append(row_of(b[s], k))
                b[s] = b[s] - m * b_rows[k]
            inv.append(r)
            known.append(seen)
        diag.append(d)
        if s + 2 < tiles:
            turned = jnp.transpose(a[s] * e)
        for i in range(s + 1, tiles):
            if i == s + 1:
                cols = [column_of(a[i], 8 * s + k) for k in range(8)]
            for k in range(8):
                if i == s + 1:
                    m = cols[k] * inv[k]
                    for q in range(k + 1, 8):
                        cols[q] = cols[q] - m * known[k][q]
                else:
                    m = column_of(turned[8 * i : 8 * i + 8, :], k)
                a[i] = a[i] - m * a_rows[k]
                if b is not None:
                    b[i] = b[i] - m * b_rows[k]
    scale = []
    for d in diag:
        y = lax.rsqrt(d)
        scale.append(y * (1.5 - 0.5 * d * y * y))
    return a, b, scale


def split(x):
    hi = x.astype(BF16)
    return hi, (x - hi.astype(F32)).astype(BF16)


def factor_kernel(count, n_feat, all_ref, s1_ref, s2_ref, c_ref, o_ref, fa_ref, fb_ref, a_ref, u_ref, l_ref):
    n_tm, chunks = all_ref.shape[:2]
    padded = s1_ref.shape[0]
    blocks = padded // 128
    halves = -(-count // 128)
    lanes = halves * 128
    groups = chunks // halves
    modes = 8 * groups
    tm = lax.axis_index("tm")

    def coeffs(g):
        return jnp.concatenate(
            [
                jnp.concatenate([all_ref[g, i * halves + h] for h in range(halves)], axis=1)
                for i in range(groups)
            ],
            axis=0,
        )

    c_ref[...] = coeffs(tm)[:, :count]
    lane = lax.broadcasted_iota(jnp.int32, (modes, lanes), 1)
    top = lax.broadcasted_iota(jnp.int32, (modes, lanes), 0)
    ones = jnp.where(jnp.logical_and(lane < count, top == 0), 1.0, 0.0).astype(BF16)
    for g in range(n_tm):
        c = coeffs(g)
        hi = c.astype(BF16)
        rest = c - hi.astype(F32)
        mid = rest.astype(BF16)
        low = (rest - mid.astype(F32)).astype(BF16)
        stack = jnp.concatenate([hi, mid, low, ones], axis=0)
        f1 = jnp.dot(s1_ref[...], stack, preferred_element_type=F32)
        f2 = jnp.dot(s2_ref[...], stack, preferred_element_type=F32)
        fh, fl = split(f1 * f2)
        at = [pl.ds((part * n_tm + g) * lanes, lanes) for part in range(3)]
        fa_ref[:, at[0]] = fh
        fa_ref[:, at[1]] = fh
        fa_ref[:, at[2]] = fl
        fb_ref[:, at[0]] = fh
        fb_ref[:, at[1]] = fl
        fb_ref[:, at[2]] = fh

    share_of = 1.0 / (count * n_tm)
    for j in range(blocks):
        gram = lax.dot_general(
            fa_ref[pl.ds(j * 128, 128), :], fb_ref[pl.ds(j * 128, padded - j * 128), :], NT,
            preferred_element_type=F32,
        )
        a_ref[pl.ds(j * 128, 128), pl.ds(j * 128, padded - j * 128)] = gram * share_of

    last = (blocks - 1) * 128
    ri = lax.broadcasted_iota(jnp.int32, (128, 128), 0)
    ci = lax.broadcasted_iota(jnp.int32, (128, 128), 1)
    corner = a_ref[pl.ds(last, 128), pl.ds(last, 128)]
    a_ref[pl.ds(last, 128), pl.ds(last, 128)] = corner + jnp.where(
        jnp.logical_and(ri == ci, ri + last >= n_feat), 1.0, 0.0
    )

    lane8 = lax.broadcasted_iota(jnp.int32, (8, 128), 1)
    sub8 = lax.broadcasted_iota(jnp.int32, (8, 128), 0)

    def block(j, carry):
        start = pl.multiple_of(j * 128, 128)
        a = [a_ref[pl.ds(start + 8 * i, 8), pl.ds(start, 128)] for i in range(16)]
        b = [jnp.where(lane8 == sub8 + 8 * i, 1.0, 0.0) for i in range(16)]
        a, b, scale = eliminate(a, b)
        for i in range(16):
            u_ref[pl.ds(8 * i, 8), :] = jnp.where(lane8 >= sub8 + 8 * i, a[i] * scale[i], 0.0)
            l_ref[pl.ds(8 * i, 8), :] = b[i] * scale[i]

        for jj in range(blocks - 1):
            @pl.when(j == jj)
            def _():
                here, after = jj * 128, (jj + 1) * 128
                if jj > 0:
                    o_ref[pl.ds(here, 128), pl.ds(0, here)] = jnp.zeros((128, here), F32)
                o_ref[pl.ds(here, 128), pl.ds(here, 128)] = u_ref[...]
                lh, ll = split(l_ref[...])
                ah, al = split(a_ref[pl.ds(here, 128), pl.ds(after, padded - after)])
                w = jnp.dot(
                    jnp.concatenate([lh, lh, ll], axis=1), jnp.concatenate([ah, al, ah], axis=0),
                    preferred_element_type=F32,
                )
                wh, wl = split(w)
                left, right = jnp.concatenate([wh, wh, wl], axis=0), jnp.concatenate([wh, wl, wh], axis=0)
                o_ref[pl.ds(here, 128), pl.ds(after, n_feat - after)] = w[:, : n_feat - after]
                for i in range(jj + 1, blocks):
                    row = i * 128
                    a_ref[pl.ds(row, 128), pl.ds(row, padded - row)] -= lax.dot_general(
                        left[:, row - after : row - after + 128], right[:, row - after :], TN,
                        preferred_element_type=F32,
                    )
        return carry

    lax.fori_loop(0, blocks - 1, block, 0)
    left = n_feat - last
    tiles = -(-left // 8)
    a = [a_ref[pl.ds(last + 8 * i, 8), pl.ds(last, 128)] for i in range(tiles)]
    a, _, scale = eliminate(a, None)
    for i in range(tiles):
        u_ref[pl.ds(8 * i, 8), :] = jnp.where(lane8 >= sub8 + 8 * i, a[i] * scale[i], 0.0)
    o_ref[pl.ds(last, left), pl.ds(0, last)] = jnp.zeros((left, last), F32)
    o_ref[pl.ds(last, left), pl.ds(last, left)] = u_ref[pl.ds(0, left), pl.ds(0, left)]


def selections(modes):
    first, second = np.triu_indices(modes)
    n_feat = 1 + modes + len(first)
    padded = -(-n_feat // 128) * 128
    one = 3 * modes
    s1 = np.zeros((padded, 4 * modes), np.float32)
    s2 = np.zeros((padded, 4 * modes), np.float32)
    s1[0, one] = s2[0, one] = 1.0
    for part in range(3):
        for m in range(modes):
            s1[1 + m, part * modes + m] = 1.0
        s1[1 + modes + np.arange(len(first)), part * modes + first] = 1.0
        s2[1 + modes + np.arange(len(first)), part * modes + second] = 1.0
    s2[1 : 1 + modes, one] = 1.0
    return n_feat, padded, s1, s2


def factorize(shared, count, modes):
    n_tm = shared.shape[0]
    n_feat, padded, s1, s2 = selections(modes)
    lanes = -(-count // 128) * 128
    vmem = pl.BlockSpec(memory_space=pltpu.VMEM)
    return pl.pallas_call(
        functools.partial(factor_kernel, count, n_feat),
        out_shape=(
            jax.ShapeDtypeStruct((modes, count), F32),
            jax.ShapeDtypeStruct((n_feat, n_feat), F32),
        ),
        in_specs=[vmem] * 3,
        out_specs=(vmem, vmem),
        scratch_shapes=[
            pltpu.VMEM((padded, 3 * n_tm * lanes), BF16),
            pltpu.VMEM((padded, 3 * n_tm * lanes), BF16),
            pltpu.VMEM((padded, padded), F32),
            pltpu.VMEM((128, 128), F32),
            pltpu.VMEM((128, 128), F32),
        ],
        compiler_params=pltpu.CompilerParams(vmem_limit_bytes=48 * 2**20),
        name="factorize",
    )(shared, jnp.asarray(s1, BF16), jnp.asarray(s2, BF16))


def body(snapshots, picks, basis, kappa):
    n_tm, n_space = lax.axis_size("tm"), lax.axis_size("space")
    modes, count = basis.shape[0], picks.shape[0]
    shared = gather_coefficients(snapshots, basis, kappa, picks.reshape(1, count), n_tm, n_space)
    coefficients, factor = factorize(shared, count, modes)
    return coefficients.T, factor


def solution(mesh):
    in_specs = (
        P("tm", None, "space", None, None),
        P("tm"),
        P(None, None, "space", None, None),
        P(None, "space", None, None),
    )
    out_specs = (P("tm", None), P())
    return jax.shard_map(body, mesh=mesh, in_specs=in_specs, out_specs=out_specs, check_vma=False)
```

```python
import functools

import jax
import jax.numpy as jnp
import numpy as np
from jax import lax
from jax.experimental import pallas as pl
from jax.experimental.pallas import tpu as pltpu
from jax.sharding import PartitionSpec as P

MESH = pl.DeviceIdType.MESH
HIGHEST = lax.Precision.HIGHEST
NT = (((1,), (1,)), ((), ()))
TN = (((0,), (0,)), ((), ()))
CHUNK = 128
F32 = jnp.float32
BF16 = jnp.bfloat16


def gather_kernel(
    n_tm, n_space, chunks, s_any, b_any, k_any, picks_ref, all_ref,
    s_ref, b_ref, k_ref, g_ref, z_ref, hb_ref, hk_ref, own_ref, land_ref,
    load, load_b, load_k, send_b, recv_b, send_k, recv_k, send_f, recv_f, send1, recv1, send2, recv2,
):
    count, nv, nx, ny, nz = s_any.shape
    modes = b_any.shape[0]
    wide, half = modes * ny, modes // 2
    taken = picks_ref.shape[1]
    rows_all = s_ref.shape[0]
    tm = lax.axis_index("tm")
    sp = lax.axis_index("space")
    core = lax.rem(tm, 2)
    sibling = tm + 1 - 2 * core
    me = tm * n_space + sp
    total = n_tm * n_space

    def peer(i):
        other = lax.rem(me + i, total)
        return other // n_space, lax.rem(other, n_space)

    loading_b = pltpu.make_async_copy(b_any, b_ref, load_b)
    loading_k = pltpu.make_async_copy(k_any, k_ref, load_k)
    loading_b.start()
    loading_k.start()
    loading = pltpu.make_async_copy(s_any, s_ref.at[pl.ds(0, count)], load)
    loading.start()
    barrier = pltpu.get_barrier_semaphore()

    def greet(i, carry):
        pl.semaphore_signal(barrier, inc=1, device_id=peer(i), device_id_type=MESH)
        return carry

    lax.fori_loop(1, total, greet, 0)
    pl.semaphore_wait(barrier, total - 1)

    def remote(src, dst, send, recv, device):
        return pltpu.make_async_remote_copy(
            src_ref=src, dst_ref=dst, send_sem=send, recv_sem=recv,
            device_id=device, device_id_type=MESH,
        )

    def plane_copies(side):
        x = nx - 1 if side == 0 else 0
        to = lax.rem(sp + (1 if side == 0 else n_space - 1), n_space)
        mine = pl.ds(core * half, half)
        return (
            remote(b_any.at[mine, :, x], hb_ref.at[side, mine], send_b.at[side], recv_b.at[side], (tm, to)),
            remote(k_any.at[:, x], hk_ref.at[side], send_k.at[side], recv_k.at[side], (tm, to)),
        )

    def forward(side):
        mine = pl.ds(core * half, half)
        return remote(
            hb_ref.at[side, mine], hb_ref.at[side, mine], send_f.at[side], recv_f.at[side], (sibling, sp)
        )

    sends = (sp < n_space - 1, sp > 0)
    receives = (sp > 0, sp < n_space - 1)
    for side in range(2):
        @pl.when(sends[side])
        def _():
            for copy in plane_copies(side):
                copy.start()

        @pl.when(jnp.logical_not(receives[side]))
        def _():
            hb_ref[side] = jnp.zeros(hb_ref.shape[1:], BF16)
            hk_ref[side] = jnp.zeros(hk_ref.shape[1:], F32)

    def store(g, at_row, v, x):
        size = g.shape[0]
        hi = g.astype(BF16)
        lo = (g - hi.astype(F32)).astype(BF16)
        at = pl.ds((v * nx + x) * nz, nz)
        g_ref[pl.ds(at_row, size), at] = hi
        g_ref[pl.ds(wide + at_row, size), at] = lo

    def spread(plane, many):
        return jnp.broadcast_to(plane[None], (many, ny, nz)).reshape(many * ny, nz)

    loading_b.wait()
    loading_k.wait()
    yi = lax.broadcasted_iota(jnp.int32, (wide, nz), 0) % ny
    zi = lax.broadcasted_iota(jnp.int32, (wide, nz), 1)
    for v in range(nv):
        b = [b_ref[:, v, x].astype(F32).reshape(wide, nz) for x in range(nx)]
        kap = [spread(k_ref[v, x], modes) for x in range(nx)]
        w = [b[x] * kap[x] for x in range(nx)]
        for x in range(nx):
            g = b[x] * (1.0 - 6.0 * kap[x])
            if x > 0:
                g = g + w[x - 1]
            if x < nx - 1:
                g = g + w[x + 1]
            g = g + jnp.where(yi < ny - 1, pltpu.roll(w[x], wide - 1, 0), 0.0)
            g = g + jnp.where(yi > 0, pltpu.roll(w[x], 1, 0), 0.0)
            g = g + jnp.where(zi < nz - 1, pltpu.roll(w[x], nz - 1, 1), 0.0)
            g = g + jnp.where(zi > 0, pltpu.roll(w[x], 1, 1), 0.0)
            store(g, 0, v, x)

    if rows_all > count:
        s_ref[pl.ds(count, rows_all - count)] = jnp.zeros((rows_all - count,) + s_ref.shape[1:], BF16)
    loading.wait()

    yr = lax.broadcasted_iota(jnp.int32, (CHUNK * ny, wide), 0) % ny
    yc = lax.broadcasted_iota(jnp.int32, (CHUNK * ny, wide), 1) % ny

    def contract(i):
        at = pl.ds(i * CHUNK, CHUNK)
        rows = jnp.concatenate(
            [s_ref[at, v, x].reshape(CHUNK * ny, nz) for v in range(nv) for x in range(nx)], axis=1
        )
        both = lax.dot_general(rows, g_ref[...], NT, preferred_element_type=F32)
        prod = both[:, :wide] + both[:, wide:]
        return jnp.sum(jnp.where(yr == yc, prod, 0.0).reshape(CHUNK, ny, wide), axis=1)

    def inner(i, carry):
        z_ref[pl.ds(pl.multiple_of(i * CHUNK, CHUNK), CHUNK), :] = contract(i)
        return carry

    lax.fori_loop(0, rows_all // CHUNK, inner, 0)

    for side in range(2):
        @pl.when(receives[side])
        def _():
            for copy in plane_copies(side):
                copy.wait_recv()
            forward(side).start()

    def outer_modes(which):
        row = pl.multiple_of(which * (half * ny), half * ny)
        for v in range(nv):
            for side, x in ((0, 0), (1, nx - 1)):
                plane = hb_ref[side, pl.ds(which * half, half), v].astype(F32).reshape(half * ny, nz)
                store(plane * spread(hk_ref[side, v], half), row, v, x)

    outer_modes(core)
    for side in range(2):
        @pl.when(receives[side])
        def _():
            forward(side).wait_recv()
    outer_modes(1 - core)

    def outer(i, carry):
        z_ref[pl.ds(pl.multiple_of(i * CHUNK, CHUNK), CHUNK), :] += contract(i)
        return carry

    lax.fori_loop(0, rows_all // CHUNK, outer, 0)

    fold = (
        lax.broadcasted_iota(jnp.int32, (modes, wide), 1) // ny
        == lax.broadcasted_iota(jnp.int32, (modes, wide), 0)
    ).astype(F32)
    part = lax.dot_general(fold, z_ref[...], NT, precision=HIGHEST, preferred_element_type=F32)
    hot = (
        lax.broadcasted_iota(jnp.int32, (rows_all, taken), 0)
        == jnp.broadcast_to(picks_ref[...], (rows_all, taken))
    ).astype(F32)
    mine = jnp.dot(part, hot, precision=HIGHEST, preferred_element_type=F32)
    halves = -(-taken // 128)
    for i in range(modes // 8):
        for h in range(halves):
            width = min(128, taken - 128 * h)
            if width < 128:
                own_ref[i * halves + h] = jnp.zeros((8, 128), F32)
            own_ref[i * halves + h, :, pl.ds(0, width)] = mine[8 * i : 8 * i + 8, 128 * h : 128 * h + width]

    def part_to(owner):
        return remote(own_ref.at[owner], land_ref.at[sp], send1.at[owner], recv1.at[sp], (tm, owner))

    for owner in range(chunks):
        @pl.when(sp != owner)
        def _():
            part_to(owner).start()

    def give_to(i):
        return remote(
            all_ref.at[tm, sp], all_ref.at[tm, sp], send2.at[i], recv2.at[tm * chunks + sp], peer(i)
        )

    @pl.when(sp < chunks)
    def _():
        land_ref[sp] = own_ref[sp]
        for source in range(n_space):
            @pl.when(sp != source)
            def _():
                remote(
                    own_ref.at[0], land_ref.at[source], send1.at[0], recv1.at[source], (tm, source)
                ).wait_recv()
        total_sum = land_ref[0]
        for source in range(1, n_space):
            total_sum = total_sum + land_ref[source]
        all_ref[tm, sp] = total_sum

        def give(i, carry):
            give_to(i).start()
            return carry

        lax.fori_loop(1, total, give, 0)

    for side in range(2):
        @pl.when(sends[side])
        def _():
            for copy in plane_copies(side):
                copy.wait_send()

        @pl.when(receives[side])
        def _():
            forward(side).wait_send()

    for owner in range(chunks):
        @pl.when(sp != owner)
        def _():
            part_to(owner).wait_send()

    for group in range(n_tm):
        for owner in range(chunks):
            @pl.when(jnp.logical_or(tm != group, sp != owner))
            def _():
                remote(
                    all_ref.at[group, owner], all_ref.at[group, owner],
                    send2.at[0], recv2.at[group * chunks + owner], (group, owner),
                ).wait_recv()

    @pl.when(sp < chunks)
    def _():
        def done(i, carry):
            give_to(i).wait_send()
            return carry

        lax.fori_loop(1, total, done, 0)


def gather_coefficients(snapshots, basis, kappa, picks_row, n_tm, n_space):
    count, nv, nx, ny, nz = snapshots.shape
    modes = basis.shape[0]
    chunks = (modes // 8) * -(-picks_row.shape[1] // 128)
    rows_all = -(-count // CHUNK) * CHUNK
    vmem = pl.BlockSpec(memory_space=pltpu.VMEM)
    dma = pltpu.SemaphoreType.DMA
    return pl.pallas_call(
        functools.partial(gather_kernel, n_tm, n_space, chunks),
        out_shape=jax.ShapeDtypeStruct((n_tm, chunks, 8, 128), F32),
        in_specs=[pl.BlockSpec(memory_space=pltpu.HBM)] * 3 + [vmem],
        out_specs=vmem,
        scratch_shapes=[
            pltpu.VMEM((rows_all, nv, nx, ny, nz), BF16),
            pltpu.VMEM(basis.shape, BF16),
            pltpu.VMEM(kappa.shape, F32),
            pltpu.VMEM((2 * modes * ny, nv * nx * nz), BF16),
            pltpu.VMEM((rows_all, modes * ny), F32),
            pltpu.VMEM((2, modes, nv, ny, nz), BF16),
            pltpu.VMEM((2, nv, ny, nz), F32),
            pltpu.VMEM((chunks, 8, 128), F32),
            pltpu.VMEM((n_space, 8, 128), F32),
            dma, dma, dma, dma((2,)), dma((2,)), dma((2,)), dma((2,)), dma((2,)), dma((2,)),
            dma((chunks,)), dma((n_space,)), dma((n_tm * n_space,)), dma((n_tm * chunks,)),
        ],
        compiler_params=pltpu.CompilerParams(
            collective_id=0, has_side_effects=True, vmem_limit_bytes=60 * 2**20
        ),
        name="gather_coefficients",
    )(snapshots, basis, kappa, picks_row)


def reciprocal(x):
    r = pl.reciprocal(x, approx=True)
    return r * (2.0 - x * r)


def parts_of(x):
    hi = x.astype(BF16).astype(F32)
    return hi, x - hi


def eliminate(a, b):
    tiles = len(a)
    sub = lax.broadcasted_iota(jnp.int32, (8, 128), 0)
    zero = jnp.zeros((8, 128), F32)
    row_of = lambda x, k: jnp.broadcast_to(x[k : k + 1, :], (8, 128))
    column_of = lambda x, k: jnp.broadcast_to(x[:, k : k + 1], (8, 128))
    diag = []
    for s in range(tiles):
        cols = [column_of(a[s], 8 * s + k) for k in range(8)]
        near = [column_of(a[s + 1], 8 * s + k) for k in range(8)] if s + 1 < tiles else None
        d, e = zero, zero
        for k in range(0, 8, 2):
            first, second = cols[k], cols[k + 1]
            p, q, t = row_of(first, k), row_of(first, k + 1), row_of(second, k + 1)
            rd = reciprocal(p * t - q * q)
            rp = reciprocal(p)
            weights = {}
            for n in range(k + 2, 8):
                x, y = row_of(cols[n], k), row_of(cols[n], k + 1)
                weights[n] = (t * x - q * y) * rd, (p * y - q * x) * rd
                cols[n] = cols[n] - first * weights[n][0] - second * weights[n][1]
            qp = q * rp
            r1 = p * rd
            d = jnp.where(sub == k, p, jnp.where(sub == k + 1, t - q * qp, d))
            e = jnp.where(sub == k, rp, jnp.where(sub == k + 1, r1, e))
            m0 = jnp.where(sub > k, first * rp, 0.0)
            m1 = jnp.where(sub > k + 1, (second - first * qp) * r1, 0.0)
            a0 = row_of(a[s], k)
            a[s] = a[s] - m0 * a0
            a1 = row_of(a[s], k + 1)
            a[s] = a[s] - m1 * a1
            if b is not None:
                b0 = row_of(b[s], k)
                b[s] = b[s] - m0 * b0
                b1 = row_of(b[s], k + 1)
                b[s] = b[s] - m1 * b1
            if near is not None:
                n0 = near[k] * rp
                n1 = (near[k + 1] - near[k] * qp) * r1
                for n in range(k + 2, 8):
                    near[n] = near[n] - near[k] * weights[n][0] - near[k + 1] * weights[n][1]
                a[s + 1] = a[s + 1] - n0 * a0 - n1 * a1
                if b is not None:
                    b[s + 1] = b[s + 1] - n0 * b0 - n1 * b1
        diag.append(d)
        if s + 2 < tiles:
            vh, vl = parts_of(a[s] * e)
            wide = a[s] if b is None else jnp.concatenate([a[s], b[s]], axis=1)
            uh, ul = parts_of(wide)
            delta = lax.dot_general(
                jnp.concatenate([vh, vh, vl, zero], axis=0).astype(BF16),
                jnp.concatenate([uh, ul, uh, jnp.zeros_like(uh)], axis=0).astype(BF16),
                TN, preferred_element_type=F32,
            )
            for i in range(s + 2, tiles):
                a[i] = a[i] - delta[8 * i : 8 * i + 8, :128]
                if b is not None:
                    b[i] = b[i] - delta[8 * i : 8 * i + 8, 128:]
    scale = []
    for d in diag:
        y = lax.rsqrt(d)
        scale.append(y * (1.5 - 0.5 * d * y * y))
    return a, b, scale


def split(x):
    hi = x.astype(BF16)
    return hi, (x - hi.astype(F32)).astype(BF16)


def factor_kernel(count, n_feat, all_ref, s1_ref, s2_ref, c_ref, o_ref, f_ref, fa_ref, fb_ref, a_ref, u_ref, l_ref):
    n_tm, chunks = all_ref.shape[:2]
    padded = s1_ref.shape[0]
    blocks = padded // 128
    halves = -(-count // 128)
    lanes = halves * 128
    groups = chunks // halves
    modes = 8 * groups
    tm = lax.axis_index("tm")

    def coeffs(g):
        return jnp.concatenate(
            [
                jnp.concatenate([all_ref[g, i * halves + h] for h in range(halves)], axis=1)
                for i in range(groups)
            ],
            axis=0,
        )

    c_ref[...] = coeffs(tm)[:, :count]
    lane = lax.broadcasted_iota(jnp.int32, (modes, lanes), 1)
    top = lax.broadcasted_iota(jnp.int32, (modes, lanes), 0)
    ones = jnp.where(jnp.logical_and(lane < count, top == 0), 1.0, 0.0).astype(BF16)
    squares = jnp.zeros((padded, 1), F32)
    for g in range(n_tm):
        c = coeffs(g)
        hi = c.astype(BF16)
        rest = c - hi.astype(F32)
        mid = rest.astype(BF16)
        low = (rest - mid.astype(F32)).astype(BF16)
        stack = jnp.concatenate([hi, mid, low, ones], axis=0)
        f1 = jnp.dot(s1_ref[...], stack, preferred_element_type=F32)
        f2 = jnp.dot(s2_ref[...], stack, preferred_element_type=F32)
        f = f1 * f2
        f_ref[:, pl.ds(g * lanes, lanes)] = f
        squares = squares + jnp.sum(f * f, axis=1, keepdims=True)
    inverse = jnp.where(squares > 0.0, lax.rsqrt(squares), 0.0)
    inverse = inverse * (1.5 - 0.5 * squares * inverse * inverse)
    size = squares * inverse * (1.0 / np.sqrt(count * n_tm))
    sizes = jnp.transpose(jnp.broadcast_to(size, (padded, 128)))[0:8, :]
    for g in range(n_tm):
        fh, fl = split(f_ref[:, pl.ds(g * lanes, lanes)] * inverse)
        at = [pl.ds((part * n_tm + g) * lanes, lanes) for part in range(3)]
        fa_ref[:, at[0]] = fh
        fa_ref[:, at[1]] = fh
        fa_ref[:, at[2]] = fl
        fb_ref[:, at[0]] = fh
        fb_ref[:, at[1]] = fl
        fb_ref[:, at[2]] = fh

    for j in range(blocks):
        gram = lax.dot_general(
            fa_ref[pl.ds(j * 128, 128), :], fb_ref[pl.ds(j * 128, padded - j * 128), :], NT,
            preferred_element_type=F32,
        )
        a_ref[pl.ds(j * 128, 128), pl.ds(j * 128, padded - j * 128)] = gram

    last = (blocks - 1) * 128
    ri = lax.broadcasted_iota(jnp.int32, (128, 128), 0)
    ci = lax.broadcasted_iota(jnp.int32, (128, 128), 1)
    corner = a_ref[pl.ds(last, 128), pl.ds(last, 128)]
    a_ref[pl.ds(last, 128), pl.ds(last, 128)] = corner + jnp.where(
        jnp.logical_and(ri == ci, ri + last >= n_feat), 1.0, 0.0
    )

    lane8 = lax.broadcasted_iota(jnp.int32, (8, 128), 1)
    sub8 = lax.broadcasted_iota(jnp.int32, (8, 128), 0)

    def block(j, carry):
        start = pl.multiple_of(j * 128, 128)
        a = [a_ref[pl.ds(start + 8 * i, 8), pl.ds(start, 128)] for i in range(16)]
        b = [jnp.where(lane8 == sub8 + 8 * i, 1.0, 0.0) for i in range(16)]
        a, b, scale = eliminate(a, b)
        for i in range(16):
            u_ref[pl.ds(8 * i, 8), :] = jnp.where(lane8 >= sub8 + 8 * i, a[i] * scale[i], 0.0)
            l_ref[pl.ds(8 * i, 8), :] = b[i] * scale[i]

        for jj in range(blocks - 1):
            @pl.when(j == jj)
            def _():
                here, after = jj * 128, (jj + 1) * 128
                if jj > 0:
                    o_ref[pl.ds(here, 128), pl.ds(0, here)] = jnp.zeros((128, here), F32)
                o_ref[pl.ds(here, 128), pl.ds(here, 128)] = u_ref[...] * sizes[0:1, here:after]
                lh, ll = split(l_ref[...])
                ah, al = split(a_ref[pl.ds(here, 128), pl.ds(after, padded - after)])
                w = jnp.dot(
                    jnp.concatenate([lh, lh, ll], axis=1), jnp.concatenate([ah, al, ah], axis=0),
                    preferred_element_type=F32,
                )
                wh, wl = split(w)
                left, right = jnp.concatenate([wh, wh, wl], axis=0), jnp.concatenate([wh, wl, wh], axis=0)
                o_ref[pl.ds(here, 128), pl.ds(after, n_feat - after)] = (
                    w[:, : n_feat - after] * sizes[0:1, after:n_feat]
                )
                for i in range(jj + 1, blocks):
                    row = i * 128
                    a_ref[pl.ds(row, 128), pl.ds(row, padded - row)] -= lax.dot_general(
                        left[:, row - after : row - after + 128], right[:, row - after :], TN,
                        preferred_element_type=F32,
                    )
        return carry

    lax.fori_loop(0, blocks - 1, block, 0)
    left = n_feat - last
    tiles = -(-left // 8)
    a = [a_ref[pl.ds(last + 8 * i, 8), pl.ds(last, 128)] for i in range(tiles)]
    a, _, scale = eliminate(a, None)
    for i in range(tiles):
        u_ref[pl.ds(8 * i, 8), :] = jnp.where(lane8 >= sub8 + 8 * i, a[i] * scale[i], 0.0)
    o_ref[pl.ds(last, left), pl.ds(0, last)] = jnp.zeros((left, last), F32)
    o_ref[pl.ds(last, left), pl.ds(last, left)] = u_ref[pl.ds(0, left), pl.ds(0, left)] * sizes[0:1, last:n_feat]


def selections(modes):
    first, second = np.triu_indices(modes)
    n_feat = 1 + modes + len(first)
    padded = -(-n_feat // 128) * 128
    one = 3 * modes
    s1 = np.zeros((padded, 4 * modes), np.float32)
    s2 = np.zeros((padded, 4 * modes), np.float32)
    s1[0, one] = s2[0, one] = 1.0
    for part in range(3):
        for m in range(modes):
            s1[1 + m, part * modes + m] = 1.0
        s1[1 + modes + np.arange(len(first)), part * modes + first] = 1.0
        s2[1 + modes + np.arange(len(first)), part * modes + second] = 1.0
    s2[1 : 1 + modes, one] = 1.0
    return n_feat, padded, s1, s2


def factorize(shared, count, modes):
    n_tm = shared.shape[0]
    n_feat, padded, s1, s2 = selections(modes)
    lanes = -(-count // 128) * 128
    vmem = pl.BlockSpec(memory_space=pltpu.VMEM)
    return pl.pallas_call(
        functools.partial(factor_kernel, count, n_feat),
        out_shape=(
            jax.ShapeDtypeStruct((modes, count), F32),
            jax.ShapeDtypeStruct((n_feat, n_feat), F32),
        ),
        in_specs=[vmem] * 3,
        out_specs=(vmem, vmem),
        scratch_shapes=[
            pltpu.VMEM((padded, n_tm * lanes), F32),
            pltpu.VMEM((padded, 3 * n_tm * lanes), BF16),
            pltpu.VMEM((padded, 3 * n_tm * lanes), BF16),
            pltpu.VMEM((padded, padded), F32),
            pltpu.VMEM((128, 128), F32),
            pltpu.VMEM((128, 128), F32),
        ],
        compiler_params=pltpu.CompilerParams(vmem_limit_bytes=60 * 2**20),
        name="factorize",
    )(shared, jnp.asarray(s1, BF16), jnp.asarray(s2, BF16))


def body(snapshots, picks, basis, kappa):
    n_tm, n_space = lax.axis_size("tm"), lax.axis_size("space")
    modes, count = basis.shape[0], picks.shape[0]
    shared = gather_coefficients(snapshots, basis, kappa, picks.reshape(1, count), n_tm, n_space)
    coefficients, factor = factorize(shared, count, modes)
    return coefficients.T, factor


def solution(mesh):
    in_specs = (
        P("tm", None, "space", None, None),
        P("tm"),
        P(None, None, "space", None, None),
        P(None, "space", None, None),
    )
    out_specs = (P("tm", None), P())
    return jax.shard_map(body, mesh=mesh, in_specs=in_specs, out_specs=out_specs, check_vma=False)
```

```python
import functools

import jax
import jax.numpy as jnp
import numpy as np
from jax import lax
from jax.experimental import pallas as pl
from jax.experimental.pallas import tpu as pltpu
from jax.sharding import PartitionSpec as P

MESH = pl.DeviceIdType.MESH
HIGHEST = lax.Precision.HIGHEST
NT = (((1,), (1,)), ((), ()))
TN = (((0,), (0,)), ((), ()))
CHUNK = 128
F32 = jnp.float32
BF16 = jnp.bfloat16


def thirds(x):
    hi = x.astype(BF16)
    rest = x - hi.astype(F32)
    mid = rest.astype(BF16)
    return hi, mid, (rest - mid.astype(F32)).astype(BF16)


def gather_kernel(
    n_tm, n_space, chunks, s_any, b_any, k_any, picks_ref, all_ref,
    s_ref, b_ref, k_ref, g_ref, z_ref, hb_ref, hk_ref, own_ref, land_ref,
    load, load_b, load_k, send_b, recv_b, send_k, recv_k, send_f, recv_f, send1, recv1, send2, recv2, send3, recv3,
):
    count, nv, nx, ny, nz = s_any.shape
    modes = b_any.shape[0]
    wide, half = modes * ny, modes // 2
    taken = picks_ref.shape[1]
    rows_all = s_ref.shape[0]
    tm = lax.axis_index("tm")
    sp = lax.axis_index("space")
    core = lax.rem(tm, 2)
    sibling = tm + 1 - 2 * core
    column = lax.div(tm, 2)
    me = column * n_space + sp
    total = (n_tm // 2) * n_space

    def peer(i):
        other = lax.rem(me + i, total)
        return 2 * lax.div(other, n_space) + core, lax.rem(other, n_space)

    loading_b = pltpu.make_async_copy(b_any, b_ref, load_b)
    loading_k = pltpu.make_async_copy(k_any, k_ref, load_k)
    loading_b.start()
    loading_k.start()
    loading = pltpu.make_async_copy(s_any, s_ref.at[pl.ds(0, count)], load)
    loading.start()
    barrier = pltpu.get_barrier_semaphore()

    def greet(i, carry):
        pl.semaphore_signal(barrier, inc=1, device_id=peer(i), device_id_type=MESH)
        return carry

    lax.fori_loop(1, total, greet, 0)
    pl.semaphore_signal(barrier, inc=1, device_id=(sibling, sp), device_id_type=MESH)
    pl.semaphore_wait(barrier, total)

    def remote(src, dst, send, recv, device):
        return pltpu.make_async_remote_copy(
            src_ref=src, dst_ref=dst, send_sem=send, recv_sem=recv,
            device_id=device, device_id_type=MESH,
        )

    def plane_copies(side):
        x = nx - 1 if side == 0 else 0
        to = lax.rem(sp + (1 if side == 0 else n_space - 1), n_space)
        mine = pl.ds(core * half, half)
        return (
            remote(b_any.at[mine, :, x], hb_ref.at[side, mine], send_b.at[side], recv_b.at[side], (tm, to)),
            remote(k_any.at[:, x], hk_ref.at[side], send_k.at[side], recv_k.at[side], (tm, to)),
        )

    def forward(side):
        mine = pl.ds(core * half, half)
        return remote(
            hb_ref.at[side, mine], hb_ref.at[side, mine], send_f.at[side], recv_f.at[side], (sibling, sp)
        )

    sends = (sp < n_space - 1, sp > 0)
    receives = (sp > 0, sp < n_space - 1)
    for side in range(2):
        @pl.when(sends[side])
        def _():
            for copy in plane_copies(side):
                copy.start()

        @pl.when(jnp.logical_not(receives[side]))
        def _():
            hb_ref[side] = jnp.zeros(hb_ref.shape[1:], BF16)
            hk_ref[side] = jnp.zeros(hk_ref.shape[1:], F32)

    def store(g, at_row, v, x):
        size = g.shape[0]
        hi = g.astype(BF16)
        lo = (g - hi.astype(F32)).astype(BF16)
        at = pl.ds((v * nx + x) * nz, nz)
        g_ref[pl.ds(at_row, size), at] = hi
        g_ref[pl.ds(wide + at_row, size), at] = lo

    def spread(plane, many):
        return jnp.broadcast_to(plane[None], (many, ny, nz)).reshape(many * ny, nz)

    loading_b.wait()
    loading_k.wait()
    yi = lax.broadcasted_iota(jnp.int32, (wide, nz), 0) % ny
    zi = lax.broadcasted_iota(jnp.int32, (wide, nz), 1)
    for v in range(nv):
        b = [b_ref[:, v, x].astype(F32).reshape(wide, nz) for x in range(nx)]
        kap = [spread(k_ref[v, x], modes) for x in range(nx)]
        w = [b[x] * kap[x] for x in range(nx)]
        for x in range(nx):
            g = b[x] * (1.0 - 6.0 * kap[x])
            if x > 0:
                g = g + w[x - 1]
            if x < nx - 1:
                g = g + w[x + 1]
            g = g + jnp.where(yi < ny - 1, pltpu.roll(w[x], wide - 1, 0), 0.0)
            g = g + jnp.where(yi > 0, pltpu.roll(w[x], 1, 0), 0.0)
            g = g + jnp.where(zi < nz - 1, pltpu.roll(w[x], nz - 1, 1), 0.0)
            g = g + jnp.where(zi > 0, pltpu.roll(w[x], 1, 1), 0.0)
            store(g, 0, v, x)

    if rows_all > count:
        s_ref[pl.ds(count, rows_all - count)] = jnp.zeros((rows_all - count,) + s_ref.shape[1:], BF16)
    loading.wait()

    yr = lax.broadcasted_iota(jnp.int32, (CHUNK * ny, wide), 0) % ny
    yc = lax.broadcasted_iota(jnp.int32, (CHUNK * ny, wide), 1) % ny

    def contract(i):
        at = pl.ds(i * CHUNK, CHUNK)
        rows = jnp.concatenate(
            [s_ref[at, v, x].reshape(CHUNK * ny, nz) for v in range(nv) for x in range(nx)], axis=1
        )
        both = lax.dot_general(rows, g_ref[...], NT, preferred_element_type=F32)
        prod = both[:, :wide] + both[:, wide:]
        return jnp.sum(jnp.where(yr == yc, prod, 0.0).reshape(CHUNK, ny, wide), axis=1)

    def inner(i, carry):
        z_ref[pl.ds(pl.multiple_of(i * CHUNK, CHUNK), CHUNK), :] = contract(i)
        return carry

    lax.fori_loop(0, rows_all // CHUNK, inner, 0)

    for side in range(2):
        @pl.when(receives[side])
        def _():
            for copy in plane_copies(side):
                copy.wait_recv()
            forward(side).start()

    def outer_modes(which):
        row = pl.multiple_of(which * (half * ny), half * ny)
        for v in range(nv):
            for side, x in ((0, 0), (1, nx - 1)):
                plane = hb_ref[side, pl.ds(which * half, half), v].astype(F32).reshape(half * ny, nz)
                store(plane * spread(hk_ref[side, v], half), row, v, x)

    outer_modes(core)
    for side in range(2):
        @pl.when(receives[side])
        def _():
            forward(side).wait_recv()
    outer_modes(1 - core)

    def outer(i, carry):
        z_ref[pl.ds(pl.multiple_of(i * CHUNK, CHUNK), CHUNK), :] += contract(i)
        return carry

    lax.fori_loop(0, rows_all // CHUNK, outer, 0)

    fold = (
        lax.broadcasted_iota(jnp.int32, (modes, wide), 1) // ny
        == lax.broadcasted_iota(jnp.int32, (modes, wide), 0)
    ).astype(BF16)
    part = lax.dot_general(
        jnp.concatenate([fold] * 3, axis=1), jnp.concatenate(thirds(z_ref[...]), axis=1), NT,
        preferred_element_type=F32,
    )
    hot = (
        lax.broadcasted_iota(jnp.int32, (rows_all, taken), 0)
        == jnp.broadcast_to(picks_ref[...], (rows_all, taken))
    ).astype(BF16)
    mine = jnp.dot(
        jnp.concatenate(thirds(part), axis=1), jnp.concatenate([hot] * 3, axis=0),
        preferred_element_type=F32,
    )
    halves = -(-taken // 128)
    for i in range(modes // 8):
        for h in range(halves):
            width = min(128, taken - 128 * h)
            if width < 128:
                own_ref[i * halves + h] = jnp.zeros((8, 128), F32)
            own_ref[i * halves + h, :, pl.ds(0, width)] = mine[8 * i : 8 * i + 8, 128 * h : 128 * h + width]

    def part_to(owner):
        return remote(own_ref.at[owner], land_ref.at[sp], send1.at[owner], recv1.at[sp], (tm, owner))

    for owner in range(chunks):
        @pl.when(sp != owner)
        def _():
            part_to(owner).start()

    def give_to(i):
        return remote(
            all_ref.at[core, column, sp], all_ref.at[core, column, sp],
            send2.at[i], recv2.at[column * chunks + sp], peer(i),
        )

    def hand_over(which):
        return remote(all_ref.at[which], all_ref.at[which], send3, recv3, (sibling, sp))

    @pl.when(sp < chunks)
    def _():
        land_ref[sp] = own_ref[sp]
        for source in range(n_space):
            @pl.when(sp != source)
            def _():
                remote(
                    own_ref.at[0], land_ref.at[source], send1.at[0], recv1.at[source], (tm, source)
                ).wait_recv()
        total_sum = land_ref[0]
        for source in range(1, n_space):
            total_sum = total_sum + land_ref[source]
        all_ref[core, column, sp] = total_sum

        def give(i, carry):
            give_to(i).start()
            return carry

        lax.fori_loop(1, total, give, 0)

    for group in range(n_tm // 2):
        for owner in range(chunks):
            @pl.when(jnp.logical_or(column != group, sp != owner))
            def _():
                remote(
                    all_ref.at[core, group, owner], all_ref.at[core, group, owner],
                    send2.at[0], recv2.at[group * chunks + owner], (2 * group + core, owner),
                ).wait_recv()

    hand_over(core).start()

    for side in range(2):
        @pl.when(sends[side])
        def _():
            for copy in plane_copies(side):
                copy.wait_send()

        @pl.when(receives[side])
        def _():
            forward(side).wait_send()

    for owner in range(chunks):
        @pl.when(sp != owner)
        def _():
            part_to(owner).wait_send()

    @pl.when(sp < chunks)
    def _():
        def done(i, carry):
            give_to(i).wait_send()
            return carry

        lax.fori_loop(1, total, done, 0)

    hand_over(core).wait_send()
    hand_over(1 - core).wait_recv()


def gather_coefficients(snapshots, basis, kappa, picks_row, n_tm, n_space):
    count, nv, nx, ny, nz = snapshots.shape
    modes = basis.shape[0]
    chunks = (modes // 8) * -(-picks_row.shape[1] // 128)
    rows_all = -(-count // CHUNK) * CHUNK
    vmem = pl.BlockSpec(memory_space=pltpu.VMEM)
    dma = pltpu.SemaphoreType.DMA
    return pl.pallas_call(
        functools.partial(gather_kernel, n_tm, n_space, chunks),
        out_shape=jax.ShapeDtypeStruct((2, n_tm // 2, chunks, 8, 128), F32),
        in_specs=[pl.BlockSpec(memory_space=pltpu.HBM)] * 3 + [vmem],
        out_specs=vmem,
        scratch_shapes=[
            pltpu.VMEM((rows_all, nv, nx, ny, nz), BF16),
            pltpu.VMEM(basis.shape, BF16),
            pltpu.VMEM(kappa.shape, F32),
            pltpu.VMEM((2 * modes * ny, nv * nx * nz), BF16),
            pltpu.VMEM((rows_all, modes * ny), F32),
            pltpu.VMEM((2, modes, nv, ny, nz), BF16),
            pltpu.VMEM((2, nv, ny, nz), F32),
            pltpu.VMEM((chunks, 8, 128), F32),
            pltpu.VMEM((n_space, 8, 128), F32),
            dma, dma, dma, dma((2,)), dma((2,)), dma((2,)), dma((2,)), dma((2,)), dma((2,)),
            dma((chunks,)), dma((n_space,)), dma((n_tm // 2 * n_space,)), dma((n_tm // 2 * chunks,)),
            dma, dma,
        ],
        compiler_params=pltpu.CompilerParams(
            collective_id=0, has_side_effects=True, vmem_limit_bytes=60 * 2**20
        ),
        name="gather_coefficients",
    )(snapshots, basis, kappa, picks_row)


def reciprocal(x):
    r = pl.reciprocal(x, approx=True)
    return r * (2.0 - x * r)


def parts_of(x):
    hi = x.astype(BF16).astype(F32)
    return hi, x - hi


def eliminate(a, b):
    tiles = len(a)
    sub = lax.broadcasted_iota(jnp.int32, (8, 128), 0)
    zero = jnp.zeros((8, 128), F32)
    row_of = lambda x, k: jnp.broadcast_to(x[k : k + 1, :], (8, 128))
    column_of = lambda x, k: jnp.broadcast_to(x[:, k : k + 1], (8, 128))
    diag = []
    for s in range(tiles):
        cols = [column_of(a[s], 8 * s + k) for k in range(8)]
        near = [column_of(a[s + 1], 8 * s + k) for k in range(8)] if s + 1 < tiles else None
        d, e = zero, zero
        for k in range(0, 8, 2):
            first, second = cols[k], cols[k + 1]
            p, q, t = row_of(first, k), row_of(first, k + 1), row_of(second, k + 1)
            rd = reciprocal(p * t - q * q)
            rp = reciprocal(p)
            weights = {}
            for n in range(k + 2, 8):
                x, y = row_of(cols[n], k), row_of(cols[n], k + 1)
                weights[n] = (t * x - q * y) * rd, (p * y - q * x) * rd
                cols[n] = cols[n] - first * weights[n][0] - second * weights[n][1]
            qp = q * rp
            r1 = p * rd
            d = jnp.where(sub == k, p, jnp.where(sub == k + 1, t - q * qp, d))
            e = jnp.where(sub == k, rp, jnp.where(sub == k + 1, r1, e))
            m0 = jnp.where(sub > k, first * rp, 0.0)
            m1 = jnp.where(sub > k + 1, (second - first * qp) * r1, 0.0)
            a0 = row_of(a[s], k)
            a[s] = a[s] - m0 * a0
            a1 = row_of(a[s], k + 1)
            a[s] = a[s] - m1 * a1
            if b is not None:
                b0 = row_of(b[s], k)
                b[s] = b[s] - m0 * b0
                b1 = row_of(b[s], k + 1)
                b[s] = b[s] - m1 * b1
            if near is not None:
                n0 = near[k] * rp
                n1 = (near[k + 1] - near[k] * qp) * r1
                for n in range(k + 2, 8):
                    near[n] = near[n] - near[k] * weights[n][0] - near[k + 1] * weights[n][1]
                a[s + 1] = a[s + 1] - n0 * a0 - n1 * a1
                if b is not None:
                    b[s + 1] = b[s + 1] - n0 * b0 - n1 * b1
        diag.append(d)
        if s + 2 < tiles:
            vh, vl = parts_of(a[s] * e)
            wide = a[s] if b is None else jnp.concatenate([a[s], b[s]], axis=1)
            uh, ul = parts_of(wide)
            delta = lax.dot_general(
                jnp.concatenate([vh, vh, vl, zero], axis=0).astype(BF16),
                jnp.concatenate([uh, ul, uh, jnp.zeros_like(uh)], axis=0).astype(BF16),
                TN, preferred_element_type=F32,
            )
            for i in range(s + 2, tiles):
                a[i] = a[i] - delta[8 * i : 8 * i + 8, :128]
                if b is not None:
                    b[i] = b[i] - delta[8 * i : 8 * i + 8, 128:]
    scale = []
    for d in diag:
        y = lax.rsqrt(d)
        scale.append(y * (1.5 - 0.5 * d * y * y))
    return a, b, scale


def split(x):
    hi = x.astype(BF16)
    return hi, (x - hi.astype(F32)).astype(BF16)


def factor_kernel(count, n_feat, all_ref, s1_ref, s2_ref, c_ref, o_ref, f_ref, fa_ref, fb_ref, a_ref, u_ref, l_ref):
    n_tm, chunks = 2 * all_ref.shape[1], all_ref.shape[2]
    padded = s1_ref.shape[0]
    blocks = padded // 128
    halves = -(-count // 128)
    lanes = halves * 128
    groups = chunks // halves
    modes = 8 * groups
    tm = lax.axis_index("tm")

    def coeffs(core, column):
        return jnp.concatenate(
            [
                jnp.concatenate([all_ref[core, column, i * halves + h] for h in range(halves)], axis=1)
                for i in range(groups)
            ],
            axis=0,
        )

    c_ref[...] = coeffs(lax.rem(tm, 2), lax.div(tm, 2))[:, :count]
    lane = lax.broadcasted_iota(jnp.int32, (modes, lanes), 1)
    top = lax.broadcasted_iota(jnp.int32, (modes, lanes), 0)
    ones = jnp.where(jnp.logical_and(lane < count, top == 0), 1.0, 0.0).astype(BF16)
    squares = jnp.zeros((padded, 1), F32)
    for g in range(n_tm):
        c = coeffs(g % 2, g // 2)
        stack = jnp.concatenate([*thirds(c), ones], axis=0)
        f1 = jnp.dot(s1_ref[...], stack, preferred_element_type=F32)
        f2 = jnp.dot(s2_ref[...], stack, preferred_element_type=F32)
        f = f1 * f2
        f_ref[:, pl.ds(g * lanes, lanes)] = f
        squares = squares + jnp.sum(f * f, axis=1, keepdims=True)
    inverse = jnp.where(squares > 0.0, lax.rsqrt(squares), 0.0)
    inverse = inverse * (1.5 - 0.5 * squares * inverse * inverse)
    size = squares * inverse * (1.0 / np.sqrt(count * n_tm))
    sizes = jnp.transpose(jnp.broadcast_to(size, (padded, 128)))[0:8, :]
    for g in range(n_tm):
        fh, fl = split(f_ref[:, pl.ds(g * lanes, lanes)] * inverse)
        at = [pl.ds((part * n_tm + g) * lanes, lanes) for part in range(3)]
        fa_ref[:, at[0]] = fh
        fa_ref[:, at[1]] = fh
        fa_ref[:, at[2]] = fl
        fb_ref[:, at[0]] = fh
        fb_ref[:, at[1]] = fl
        fb_ref[:, at[2]] = fh

    for col in range(0, padded, 256):
        end = min(col + 256, padded)
        a_ref[pl.ds(0, end), pl.ds(col, end - col)] = lax.dot_general(
            fa_ref[pl.ds(0, end), :], fb_ref[pl.ds(col, end - col), :], NT,
            preferred_element_type=F32,
        )

    last = (blocks - 1) * 128
    ri = lax.broadcasted_iota(jnp.int32, (128, 128), 0)
    ci = lax.broadcasted_iota(jnp.int32, (128, 128), 1)
    corner = a_ref[pl.ds(last, 128), pl.ds(last, 128)]
    a_ref[pl.ds(last, 128), pl.ds(last, 128)] = corner + jnp.where(
        jnp.logical_and(ri == ci, ri + last >= n_feat), 1.0, 0.0
    )

    lane8 = lax.broadcasted_iota(jnp.int32, (8, 128), 1)
    sub8 = lax.broadcasted_iota(jnp.int32, (8, 128), 0)

    def block(j, carry):
        start = pl.multiple_of(j * 128, 128)
        a = [a_ref[pl.ds(start + 8 * i, 8), pl.ds(start, 128)] for i in range(16)]
        b = [jnp.where(lane8 == sub8 + 8 * i, 1.0, 0.0) for i in range(16)]
        a, b, scale = eliminate(a, b)
        for i in range(16):
            u_ref[pl.ds(8 * i, 8), :] = jnp.where(lane8 >= sub8 + 8 * i, a[i] * scale[i], 0.0)
            l_ref[pl.ds(8 * i, 8), :] = b[i] * scale[i]

        for jj in range(blocks - 1):
            @pl.when(j == jj)
            def _():
                here, after = jj * 128, (jj + 1) * 128
                if jj > 0:
                    o_ref[pl.ds(here, 128), pl.ds(0, here)] = jnp.zeros((128, here), F32)
                o_ref[pl.ds(here, 128), pl.ds(here, 128)] = u_ref[...] * sizes[0:1, here:after]
                lh, ll = split(l_ref[...])
                ah, al = split(a_ref[pl.ds(here, 128), pl.ds(after, padded - after)])
                w = jnp.dot(
                    jnp.concatenate([lh, lh, ll], axis=1), jnp.concatenate([ah, al, ah], axis=0),
                    preferred_element_type=F32,
                )
                wh, wl = split(w)
                left, right = jnp.concatenate([wh, wh, wl], axis=0), jnp.concatenate([wh, wl, wh], axis=0)
                o_ref[pl.ds(here, 128), pl.ds(after, n_feat - after)] = (
                    w[:, : n_feat - after] * sizes[0:1, after:n_feat]
                )
                for col in range(after, padded, 256):
                    end = min(col + 256, padded)
                    a_ref[pl.ds(after, end - after), pl.ds(col, end - col)] -= lax.dot_general(
                        left[:, : end - after], right[:, col - after : end - after], TN,
                        preferred_element_type=F32,
                    )
        return carry

    lax.fori_loop(0, blocks - 1, block, 0)
    left = n_feat - last
    tiles = -(-left // 8)
    a = [a_ref[pl.ds(last + 8 * i, 8), pl.ds(last, 128)] for i in range(tiles)]
    a, _, scale = eliminate(a, None)
    for i in range(tiles):
        u_ref[pl.ds(8 * i, 8), :] = jnp.where(lane8 >= sub8 + 8 * i, a[i] * scale[i], 0.0)
    o_ref[pl.ds(last, left), pl.ds(0, last)] = jnp.zeros((left, last), F32)
    o_ref[pl.ds(last, left), pl.ds(last, left)] = u_ref[pl.ds(0, left), pl.ds(0, left)] * sizes[0:1, last:n_feat]


def selections(modes):
    first, second = np.triu_indices(modes)
    n_feat = 1 + modes + len(first)
    padded = -(-n_feat // 128) * 128
    one = 3 * modes
    s1 = np.zeros((padded, 4 * modes), np.float32)
    s2 = np.zeros((padded, 4 * modes), np.float32)
    s1[0, one] = s2[0, one] = 1.0
    for part in range(3):
        for m in range(modes):
            s1[1 + m, part * modes + m] = 1.0
        s1[1 + modes + np.arange(len(first)), part * modes + first] = 1.0
        s2[1 + modes + np.arange(len(first)), part * modes + second] = 1.0
    s2[1 : 1 + modes, one] = 1.0
    return n_feat, padded, s1, s2


def factorize(shared, count, modes):
    n_tm = 2 * shared.shape[1]
    n_feat, padded, s1, s2 = selections(modes)
    lanes = -(-count // 128) * 128
    vmem = pl.BlockSpec(memory_space=pltpu.VMEM)
    return pl.pallas_call(
        functools.partial(factor_kernel, count, n_feat),
        out_shape=(
            jax.ShapeDtypeStruct((modes, count), F32),
            jax.ShapeDtypeStruct((n_feat, n_feat), F32),
        ),
        in_specs=[vmem] * 3,
        out_specs=(vmem, vmem),
        scratch_shapes=[
            pltpu.VMEM((padded, n_tm * lanes), F32),
            pltpu.VMEM((padded, 3 * n_tm * lanes), BF16),
            pltpu.VMEM((padded, 3 * n_tm * lanes), BF16),
            pltpu.VMEM((padded, padded), F32),
            pltpu.VMEM((128, 128), F32),
            pltpu.VMEM((128, 128), F32),
        ],
        compiler_params=pltpu.CompilerParams(vmem_limit_bytes=60 * 2**20),
        name="factorize",
    )(shared, jnp.asarray(s1, BF16), jnp.asarray(s2, BF16))


def body(snapshots, picks, basis, kappa):
    n_tm, n_space = lax.axis_size("tm"), lax.axis_size("space")
    modes, count = basis.shape[0], picks.shape[0]
    shared = gather_coefficients(snapshots, basis, kappa, picks.reshape(1, count), n_tm, n_space)
    coefficients, factor = factorize(shared, count, modes)
    return coefficients.T, factor


def solution(mesh):
    in_specs = (
        P("tm", None, "space", None, None),
        P("tm"),
        P(None, None, "space", None, None),
        P(None, "space", None, None),
    )
    out_specs = (P("tm", None), P())
    return jax.shard_map(body, mesh=mesh, in_specs=in_specs, out_specs=out_specs, check_vma=False)
```

```python
import functools

import jax
import jax.numpy as jnp
import numpy as np
from jax import lax
from jax.experimental import pallas as pl
from jax.experimental.pallas import tpu as pltpu
from jax.sharding import PartitionSpec as P

MESH = pl.DeviceIdType.MESH
HIGHEST = lax.Precision.HIGHEST
NT = (((1,), (1,)), ((), ()))
TN = (((0,), (0,)), ((), ()))
CHUNK = 128
F32 = jnp.float32
BF16 = jnp.bfloat16


def thirds(x):
    hi = x.astype(BF16)
    rest = x - hi.astype(F32)
    mid = rest.astype(BF16)
    return hi, mid, (rest - mid.astype(F32)).astype(BF16)


def gather_kernel(
    n_tm, n_space, chunks, s_any, b_any, k_any, picks_ref, all_ref,
    s_ref, rows_ref, b_ref, k_ref, g_ref, z_ref, hb_ref, hk_ref, own_ref, land_ref,
    load, load_b, load_k, send_b, recv_b, send_k, recv_k, send_f, recv_f, send1, recv1, send2, recv2, send3, recv3,
):
    count, nv, nx, ny, nz = s_any.shape
    modes = b_any.shape[0]
    wide, half = modes * ny, modes // 2
    taken = picks_ref.shape[1]
    rows_all = s_ref.shape[0]
    tm = lax.axis_index("tm")
    sp = lax.axis_index("space")
    core = lax.rem(tm, 2)
    sibling = tm + 1 - 2 * core
    column = lax.div(tm, 2)
    me = column * n_space + sp
    total = (n_tm // 2) * n_space

    def peer(i):
        other = lax.rem(me + i, total)
        return 2 * lax.div(other, n_space) + core, lax.rem(other, n_space)

    loading_b = pltpu.make_async_copy(b_any, b_ref, load_b)
    loading_k = pltpu.make_async_copy(k_any, k_ref, load_k)
    loading_b.start()
    loading_k.start()
    loading = pltpu.make_async_copy(s_any, s_ref.at[pl.ds(0, count)], load)
    loading.start()
    barrier = pltpu.get_barrier_semaphore()

    def greet(i, carry):
        pl.semaphore_signal(barrier, inc=1, device_id=peer(i), device_id_type=MESH)
        return carry

    lax.fori_loop(1, total, greet, 0)
    pl.semaphore_signal(barrier, inc=1, device_id=(sibling, sp), device_id_type=MESH)
    pl.semaphore_wait(barrier, total)

    def remote(src, dst, send, recv, device):
        return pltpu.make_async_remote_copy(
            src_ref=src, dst_ref=dst, send_sem=send, recv_sem=recv,
            device_id=device, device_id_type=MESH,
        )

    def plane_copies(side):
        x = nx - 1 if side == 0 else 0
        to = lax.rem(sp + (1 if side == 0 else n_space - 1), n_space)
        mine = pl.ds(core * half, half)
        return (
            remote(b_any.at[mine, :, x], hb_ref.at[side, mine], send_b.at[side], recv_b.at[side], (tm, to)),
            remote(k_any.at[:, x], hk_ref.at[side], send_k.at[side], recv_k.at[side], (tm, to)),
        )

    def forward(side):
        mine = pl.ds(core * half, half)
        return remote(
            hb_ref.at[side, mine], hb_ref.at[side, mine], send_f.at[side], recv_f.at[side], (sibling, sp)
        )

    sends = (sp < n_space - 1, sp > 0)
    receives = (sp > 0, sp < n_space - 1)
    for side in range(2):
        @pl.when(sends[side])
        def _():
            for copy in plane_copies(side):
                copy.start()

        @pl.when(jnp.logical_not(receives[side]))
        def _():
            hb_ref[side] = jnp.zeros(hb_ref.shape[1:], BF16)
            hk_ref[side] = jnp.zeros(hk_ref.shape[1:], F32)

    def store(g, at_row, v, x):
        size = g.shape[0]
        hi = g.astype(BF16)
        lo = (g - hi.astype(F32)).astype(BF16)
        at = pl.ds((v * nx + x) * nz, nz)
        g_ref[pl.ds(at_row, size), at] = hi
        g_ref[pl.ds(wide + at_row, size), at] = lo

    def spread(plane, many):
        return jnp.broadcast_to(plane[None], (many, ny, nz)).reshape(many * ny, nz)

    loading_b.wait()
    loading_k.wait()
    yi = lax.broadcasted_iota(jnp.int32, (wide, nz), 0) % ny
    zi = lax.broadcasted_iota(jnp.int32, (wide, nz), 1)
    for v in range(nv):
        b = [b_ref[:, v, x].astype(F32).reshape(wide, nz) for x in range(nx)]
        kap = [spread(k_ref[v, x], modes) for x in range(nx)]
        w = [b[x] * kap[x] for x in range(nx)]
        for x in range(nx):
            g = b[x] * (1.0 - 6.0 * kap[x])
            if x > 0:
                g = g + w[x - 1]
            if x < nx - 1:
                g = g + w[x + 1]
            g = g + jnp.where(yi < ny - 1, pltpu.roll(w[x], wide - 1, 0), 0.0)
            g = g + jnp.where(yi > 0, pltpu.roll(w[x], 1, 0), 0.0)
            g = g + jnp.where(zi < nz - 1, pltpu.roll(w[x], nz - 1, 1), 0.0)
            g = g + jnp.where(zi > 0, pltpu.roll(w[x], 1, 1), 0.0)
            store(g, 0, v, x)

    if rows_all > count:
        s_ref[pl.ds(count, rows_all - count)] = jnp.zeros((rows_all - count,) + s_ref.shape[1:], BF16)
    loading.wait()

    yr = lax.broadcasted_iota(jnp.int32, (CHUNK * ny, wide), 0) % ny
    yc = lax.broadcasted_iota(jnp.int32, (CHUNK * ny, wide), 1) % ny

    def lay(i):
        at = pl.ds(i * CHUNK, CHUNK)
        return jnp.concatenate(
            [s_ref[at, v, x].reshape(CHUNK * ny, nz) for v in range(nv) for x in range(nx)], axis=1
        )

    def contract(rows):
        both = lax.dot_general(rows, g_ref[...], NT, preferred_element_type=F32)
        prod = both[:, :wide] + both[:, wide:]
        return jnp.sum(jnp.where(yr == yc, prod, 0.0).reshape(CHUNK, ny, wide), axis=1)

    def inner(i, carry):
        rows = lay(i)
        rows_ref[pl.ds(pl.multiple_of(i * CHUNK * ny, CHUNK * ny), CHUNK * ny), :] = rows
        z_ref[pl.ds(pl.multiple_of(i * CHUNK, CHUNK), CHUNK), :] = contract(rows)
        return carry

    lax.fori_loop(0, rows_all // CHUNK, inner, 0)

    for side in range(2):
        @pl.when(receives[side])
        def _():
            for copy in plane_copies(side):
                copy.wait_recv()
            forward(side).start()

    def outer_modes(which):
        row = pl.multiple_of(which * (half * ny), half * ny)
        for v in range(nv):
            for side, x in ((0, 0), (1, nx - 1)):
                plane = hb_ref[side, pl.ds(which * half, half), v].astype(F32).reshape(half * ny, nz)
                store(plane * spread(hk_ref[side, v], half), row, v, x)

    outer_modes(core)
    for side in range(2):
        @pl.when(receives[side])
        def _():
            forward(side).wait_recv()
    outer_modes(1 - core)

    def outer(i, carry):
        rows = rows_ref[pl.ds(pl.multiple_of(i * CHUNK * ny, CHUNK * ny), CHUNK * ny), :]
        z_ref[pl.ds(pl.multiple_of(i * CHUNK, CHUNK), CHUNK), :] += contract(rows)
        return carry

    lax.fori_loop(0, rows_all // CHUNK, outer, 0)

    fold = (
        lax.broadcasted_iota(jnp.int32, (modes, wide), 1) // ny
        == lax.broadcasted_iota(jnp.int32, (modes, wide), 0)
    ).astype(BF16)
    part = lax.dot_general(
        jnp.concatenate([fold] * 3, axis=1), jnp.concatenate(thirds(z_ref[...]), axis=1), NT,
        preferred_element_type=F32,
    )
    hot = (
        lax.broadcasted_iota(jnp.int32, (rows_all, taken), 0)
        == jnp.broadcast_to(picks_ref[...], (rows_all, taken))
    ).astype(BF16)
    mine = jnp.dot(
        jnp.concatenate(thirds(part), axis=1), jnp.concatenate([hot] * 3, axis=0),
        preferred_element_type=F32,
    )
    halves = -(-taken // 128)
    for i in range(modes // 8):
        for h in range(halves):
            width = min(128, taken - 128 * h)
            if width < 128:
                own_ref[i * halves + h] = jnp.zeros((8, 128), F32)
            own_ref[i * halves + h, :, pl.ds(0, width)] = mine[8 * i : 8 * i + 8, 128 * h : 128 * h + width]

    def part_to(owner):
        return remote(own_ref.at[owner], land_ref.at[sp], send1.at[owner], recv1.at[sp], (tm, owner))

    for owner in range(chunks):
        @pl.when(sp != owner)
        def _():
            part_to(owner).start()

    def give_to(i):
        return remote(
            all_ref.at[core, column, sp], all_ref.at[core, column, sp],
            send2.at[i], recv2.at[column * chunks + sp], peer(i),
        )

    def hand_over(which):
        return remote(all_ref.at[which], all_ref.at[which], send3, recv3, (sibling, sp))

    @pl.when(sp < chunks)
    def _():
        land_ref[sp] = own_ref[sp]
        for source in range(n_space):
            @pl.when(sp != source)
            def _():
                remote(
                    own_ref.at[0], land_ref.at[source], send1.at[0], recv1.at[source], (tm, source)
                ).wait_recv()
        total_sum = land_ref[0]
        for source in range(1, n_space):
            total_sum = total_sum + land_ref[source]
        all_ref[core, column, sp] = total_sum

        def give(i, carry):
            give_to(i).start()
            return carry

        lax.fori_loop(1, total, give, 0)

    for group in range(n_tm // 2):
        for owner in range(chunks):
            @pl.when(jnp.logical_or(column != group, sp != owner))
            def _():
                remote(
                    all_ref.at[core, group, owner], all_ref.at[core, group, owner],
                    send2.at[0], recv2.at[group * chunks + owner], (2 * group + core, owner),
                ).wait_recv()

    hand_over(core).start()

    for side in range(2):
        @pl.when(sends[side])
        def _():
            for copy in plane_copies(side):
                copy.wait_send()

        @pl.when(receives[side])
        def _():
            forward(side).wait_send()

    for owner in range(chunks):
        @pl.when(sp != owner)
        def _():
            part_to(owner).wait_send()

    @pl.when(sp < chunks)
    def _():
        def done(i, carry):
            give_to(i).wait_send()
            return carry

        lax.fori_loop(1, total, done, 0)

    hand_over(core).wait_send()
    hand_over(1 - core).wait_recv()


def gather_coefficients(snapshots, basis, kappa, picks_row, n_tm, n_space):
    count, nv, nx, ny, nz = snapshots.shape
    modes = basis.shape[0]
    chunks = (modes // 8) * -(-picks_row.shape[1] // 128)
    rows_all = -(-count // CHUNK) * CHUNK
    vmem = pl.BlockSpec(memory_space=pltpu.VMEM)
    dma = pltpu.SemaphoreType.DMA
    return pl.pallas_call(
        functools.partial(gather_kernel, n_tm, n_space, chunks),
        out_shape=jax.ShapeDtypeStruct((2, n_tm // 2, chunks, 8, 128), F32),
        in_specs=[pl.BlockSpec(memory_space=pltpu.HBM)] * 3 + [vmem],
        out_specs=vmem,
        scratch_shapes=[
            pltpu.VMEM((rows_all, nv, nx, ny, nz), BF16),
            pltpu.VMEM((rows_all * ny, nv * nx * nz), BF16),
            pltpu.VMEM(basis.shape, BF16),
            pltpu.VMEM(kappa.shape, F32),
            pltpu.VMEM((2 * modes * ny, nv * nx * nz), BF16),
            pltpu.VMEM((rows_all, modes * ny), F32),
            pltpu.VMEM((2, modes, nv, ny, nz), BF16),
            pltpu.VMEM((2, nv, ny, nz), F32),
            pltpu.VMEM((chunks, 8, 128), F32),
            pltpu.VMEM((n_space, 8, 128), F32),
            dma, dma, dma, dma((2,)), dma((2,)), dma((2,)), dma((2,)), dma((2,)), dma((2,)),
            dma((chunks,)), dma((n_space,)), dma((n_tm // 2 * n_space,)), dma((n_tm // 2 * chunks,)),
            dma, dma,
        ],
        compiler_params=pltpu.CompilerParams(
            collective_id=0, has_side_effects=True, vmem_limit_bytes=60 * 2**20
        ),
        name="gather_coefficients",
    )(snapshots, basis, kappa, picks_row)


def reciprocal(x):
    r = pl.reciprocal(x, approx=True)
    return r * (2.0 - x * r)


def parts_of(x):
    hi = x.astype(BF16).astype(F32)
    return hi, x - hi


def eliminate(a, b):
    tiles = len(a)
    sub = lax.broadcasted_iota(jnp.int32, (8, 128), 0)
    zero = jnp.zeros((8, 128), F32)
    row_of = lambda x, k: jnp.broadcast_to(x[k : k + 1, :], (8, 128))
    column_of = lambda x, k: jnp.broadcast_to(x[:, k : k + 1], (8, 128))
    diag = []
    for s in range(tiles):
        cols = [column_of(a[s], 8 * s + k) for k in range(8)]
        near = [column_of(a[s + 1], 8 * s + k) for k in range(8)] if s + 1 < tiles else None
        d, e = zero, zero
        for k in range(0, 8, 2):
            first, second = cols[k], cols[k + 1]
            p, q, t = row_of(first, k), row_of(first, k + 1), row_of(second, k + 1)
            rd = reciprocal(p * t - q * q)
            rp = reciprocal(p)
            weights = {}
            for n in range(k + 2, 8):
                x, y = row_of(cols[n], k), row_of(cols[n], k + 1)
                weights[n] = (t * x - q * y) * rd, (p * y - q * x) * rd
                cols[n] = cols[n] - first * weights[n][0] - second * weights[n][1]
            qp = q * rp
            r1 = p * rd
            d = jnp.where(sub == k, p, jnp.where(sub == k + 1, t - q * qp, d))
            e = jnp.where(sub == k, rp, jnp.where(sub == k + 1, r1, e))
            m0 = jnp.where(sub > k, first * rp, 0.0)
            m1 = jnp.where(sub > k + 1, (second - first * qp) * r1, 0.0)
            a0 = row_of(a[s], k)
            a[s] = a[s] - m0 * a0
            a1 = row_of(a[s], k + 1)
            a[s] = a[s] - m1 * a1
            if b is not None:
                b0 = row_of(b[s], k)
                b[s] = b[s] - m0 * b0
                b1 = row_of(b[s], k + 1)
                b[s] = b[s] - m1 * b1
            if near is not None:
                n0 = near[k] * rp
                n1 = (near[k + 1] - near[k] * qp) * r1
                for n in range(k + 2, 8):
                    near[n] = near[n] - near[k] * weights[n][0] - near[k + 1] * weights[n][1]
                a[s + 1] = a[s + 1] - n0 * a0 - n1 * a1
                if b is not None:
                    b[s + 1] = b[s + 1] - n0 * b0 - n1 * b1
        diag.append(d)
        if s + 2 < tiles:
            vh, vl = parts_of(a[s] * e)
            wide = a[s] if b is None else jnp.concatenate([a[s], b[s]], axis=1)
            uh, ul = parts_of(wide)
            delta = lax.dot_general(
                jnp.concatenate([vh, vh, vl, zero], axis=0).astype(BF16),
                jnp.concatenate([uh, ul, uh, jnp.zeros_like(uh)], axis=0).astype(BF16),
                TN, preferred_element_type=F32,
            )
            for i in range(s + 2, tiles):
                a[i] = a[i] - delta[8 * i : 8 * i + 8, :128]
                if b is not None:
                    b[i] = b[i] - delta[8 * i : 8 * i + 8, 128:]
    scale = []
    for d in diag:
        y = lax.rsqrt(d)
        scale.append(y * (1.5 - 0.5 * d * y * y))
    return a, b, scale


def split(x):
    hi = x.astype(BF16)
    return hi, (x - hi.astype(F32)).astype(BF16)


def factor_kernel(count, n_feat, all_ref, s1_ref, s2_ref, c_ref, o_ref, f_ref, fa_ref, fb_ref, a_ref, u_ref):
    n_tm, chunks = 2 * all_ref.shape[1], all_ref.shape[2]
    padded = s1_ref.shape[0]
    blocks = padded // 128
    halves = -(-count // 128)
    lanes = halves * 128
    groups = chunks // halves
    modes = 8 * groups
    tm = lax.axis_index("tm")

    def coeffs(core, column):
        return jnp.concatenate(
            [
                jnp.concatenate([all_ref[core, column, i * halves + h] for h in range(halves)], axis=1)
                for i in range(groups)
            ],
            axis=0,
        )

    c_ref[...] = coeffs(lax.rem(tm, 2), lax.div(tm, 2))[:, :count]
    lane = lax.broadcasted_iota(jnp.int32, (modes, lanes), 1)
    top = lax.broadcasted_iota(jnp.int32, (modes, lanes), 0)
    ones = jnp.where(jnp.logical_and(lane < count, top == 0), 1.0, 0.0).astype(BF16)
    squares = jnp.zeros((padded, 1), F32)
    for g in range(n_tm):
        c = coeffs(g % 2, g // 2)
        stack = jnp.concatenate([*thirds(c), ones], axis=0)
        f1 = jnp.dot(s1_ref[...], stack, preferred_element_type=F32)
        f2 = jnp.dot(s2_ref[...], stack, preferred_element_type=F32)
        f = f1 * f2
        f_ref[:, pl.ds(g * lanes, lanes)] = f
        squares = squares + jnp.sum(f * f, axis=1, keepdims=True)
    inverse = jnp.where(squares > 0.0, lax.rsqrt(squares), 0.0)
    inverse = inverse * (1.5 - 0.5 * squares * inverse * inverse)
    size = squares * inverse * (1.0 / np.sqrt(count * n_tm))
    sizes = jnp.transpose(jnp.broadcast_to(size, (padded, 128)))[0:8, :]
    for g in range(n_tm):
        fh, fl = split(f_ref[:, pl.ds(g * lanes, lanes)] * inverse)
        at = [pl.ds((part * n_tm + g) * lanes, lanes) for part in range(3)]
        fa_ref[:, at[0]] = fh
        fa_ref[:, at[1]] = fh
        fa_ref[:, at[2]] = fl
        fb_ref[:, at[0]] = fh
        fb_ref[:, at[1]] = fl
        fb_ref[:, at[2]] = fh

    for col in range(0, padded, 256):
        end = min(col + 256, padded)
        a_ref[pl.ds(0, end), pl.ds(col, end - col)] = lax.dot_general(
            fa_ref[pl.ds(0, end), :], fb_ref[pl.ds(col, end - col), :], NT,
            preferred_element_type=F32,
        )

    last = (blocks - 1) * 128
    ri = lax.broadcasted_iota(jnp.int32, (128, 128), 0)
    ci = lax.broadcasted_iota(jnp.int32, (128, 128), 1)
    corner = a_ref[pl.ds(last, 128), pl.ds(last, 128)]
    a_ref[pl.ds(last, 128), pl.ds(last, 128)] = corner + jnp.where(
        jnp.logical_and(ri == ci, ri + last >= n_feat), 1.0, 0.0
    )

    lane8 = lax.broadcasted_iota(jnp.int32, (8, 128), 1)
    sub8 = lax.broadcasted_iota(jnp.int32, (8, 128), 0)

    for j in range(blocks - 1):
        here, after = j * 128, (j + 1) * 128
        a = [a_ref[pl.ds(here + 8 * i, 8), pl.ds(here, 128)] for i in range(16)]
        b = [jnp.where(lane8 == sub8 + 8 * i, 1.0, 0.0) for i in range(16)]
        a, b, scale = eliminate(a, b)
        lh, ll = split(jnp.concatenate([b[i] * scale[i] for i in range(16)], axis=0))
        inverse_rows = jnp.concatenate([lh, lh, ll], axis=1)

        def solve(col, end):
            ah, al = split(a_ref[pl.ds(here, 128), pl.ds(col, end - col)])
            w = jnp.dot(
                inverse_rows, jnp.concatenate([ah, al, ah], axis=0), preferred_element_type=F32
            )
            stop = min(end, n_feat)
            o_ref[pl.ds(here, 128), pl.ds(col, stop - col)] = w[:, : stop - col] * sizes[0:1, col:stop]
            wh, wl = split(w)
            return jnp.concatenate([wh, wh, wl], axis=0), jnp.concatenate([wh, wl, wh], axis=0)

        def update(lhs, rhs, row, col):
            at = pl.ds(row, lhs.shape[1]), pl.ds(col, rhs.shape[1])
            a_ref[at] -= lax.dot_general(lhs, rhs, TN, preferred_element_type=F32)

        left, right = solve(after, after + 128)
        update(left, right, after, after)
        rest = after + 128
        if rest < padded:
            more_left, more_right = solve(rest, padded)
            for col in range(rest, padded, 256):
                end = min(col + 256, padded)
                update(
                    jnp.concatenate([left, more_left[:, : end - rest]], axis=1),
                    more_right[:, col - rest : end - rest], after, col,
                )
        for i in range(16):
            o_ref[pl.ds(here + 8 * i, 8), pl.ds(here, 128)] = (
                jnp.where(lane8 >= sub8 + 8 * i, a[i] * scale[i], 0.0) * sizes[0:1, here:after]
            )
        if j > 0:
            o_ref[pl.ds(here, 128), pl.ds(0, here)] = jnp.zeros((128, here), F32)

    left = n_feat - last
    tiles = -(-left // 8)
    a = [a_ref[pl.ds(last + 8 * i, 8), pl.ds(last, 128)] for i in range(tiles)]
    a, _, scale = eliminate(a, None)
    for i in range(tiles):
        u_ref[pl.ds(8 * i, 8), :] = jnp.where(lane8 >= sub8 + 8 * i, a[i] * scale[i], 0.0)
    o_ref[pl.ds(last, left), pl.ds(0, last)] = jnp.zeros((left, last), F32)
    o_ref[pl.ds(last, left), pl.ds(last, left)] = u_ref[pl.ds(0, left), pl.ds(0, left)] * sizes[0:1, last:n_feat]


def selections(modes):
    first, second = np.triu_indices(modes)
    n_feat = 1 + modes + len(first)
    padded = -(-n_feat // 128) * 128
    one = 3 * modes
    s1 = np.zeros((padded, 4 * modes), np.float32)
    s2 = np.zeros((padded, 4 * modes), np.float32)
    s1[0, one] = s2[0, one] = 1.0
    for part in range(3):
        for m in range(modes):
            s1[1 + m, part * modes + m] = 1.0
        s1[1 + modes + np.arange(len(first)), part * modes + first] = 1.0
        s2[1 + modes + np.arange(len(first)), part * modes + second] = 1.0
    s2[1 : 1 + modes, one] = 1.0
    return n_feat, padded, s1, s2


def factorize(shared, count, modes):
    n_tm = 2 * shared.shape[1]
    n_feat, padded, s1, s2 = selections(modes)
    lanes = -(-count // 128) * 128
    vmem = pl.BlockSpec(memory_space=pltpu.VMEM)
    return pl.pallas_call(
        functools.partial(factor_kernel, count, n_feat),
        out_shape=(
            jax.ShapeDtypeStruct((modes, count), F32),
            jax.ShapeDtypeStruct((n_feat, n_feat), F32),
        ),
        in_specs=[vmem] * 3,
        out_specs=(vmem, vmem),
        scratch_shapes=[
            pltpu.VMEM((padded, n_tm * lanes), F32),
            pltpu.VMEM((padded, 3 * n_tm * lanes), BF16),
            pltpu.VMEM((padded, 3 * n_tm * lanes), BF16),
            pltpu.VMEM((padded, padded), F32),
            pltpu.VMEM((128, 128), F32),
        ],
        compiler_params=pltpu.CompilerParams(vmem_limit_bytes=60 * 2**20),
        name="factorize",
    )(shared, jnp.asarray(s1, BF16), jnp.asarray(s2, BF16))


def body(snapshots, picks, basis, kappa):
    n_tm, n_space = lax.axis_size("tm"), lax.axis_size("space")
    modes, count = basis.shape[0], picks.shape[0]
    shared = gather_coefficients(snapshots, basis, kappa, picks.reshape(1, count), n_tm, n_space)
    coefficients, factor = factorize(shared, count, modes)
    return coefficients.T, factor


def solution(mesh):
    in_specs = (
        P("tm", None, "space", None, None),
        P("tm"),
        P(None, None, "space", None, None),
        P(None, "space", None, None),
    )
    out_specs = (P("tm", None), P())
    return jax.shard_map(body, mesh=mesh, in_specs=in_specs, out_specs=out_specs, check_vma=False)
```
